32 devices in a mesh: ctx: 8 (over y, x, core), tp: 4 (over z).
Axes of the slice: x: 2, y: 2, z: 4, core: 2. Of those that a mesh axis runs over, the one named last changes fastest.
Arguments:
- streams: bfloat16 [3, 2048, 2048], P(None, 'ctx', 'tp'), may hold values from -6 to 6
- short_filter: float32 [3, 7, 2048], P(None, None, 'tp'), may hold values from -2 to 2
- decay_rates: float32 [2048, 16], P('tp'), may hold values from 2.4414063e-05 to 0.05, as said below
- residues: float32 [2048, 16], P('tp'), may hold values from -0.06 to 0.06
- skip_gain: float32 [2048], P('tp'), may hold values from 0.5 to 1.5
- hyena_weight: bfloat16 [2048, 4096], P('tp'), may hold values from -0.1875 to 0.1875
- value_weight: bfloat16 [4096, 2048], P('tp'), may hold values from -0.125 to 0.125
- queries: bfloat16 [2048, 2048], P('ctx', 'tp'), may hold values from -16.5 to 16.5
- key_vectors: bfloat16 [2048, 2048], P('ctx', 'tp'), may hold values from -16.5 to 16.5
Outputs:
- hyena_out: bfloat16 [2048, 4096], P('ctx', 'tp')
- context: bfloat16 [2048, 2048], P('ctx', 'tp')
The draws below stay inside these ranges and needn't reach their ends.
Inputs may be any that keep to these rules, and one draw needn't show every extreme that they name: `decay_rates`: decay rates lie between 1 / 40960 and 0.05.
All inputs are finite; a program needn't handle non-finite values.
Results may differ from the reference program's by a relative error of at most 0.0066.
Values may be sent and summed in bfloat16 or wider, within the bound.
A program may use at most 128 MiB of HBM per device.

```python
import math
import jax
import jax.numpy as jnp
from jax import lax

D = 4096
HC = 2048
MODES = 16
HA = 16
HD = 128
SEQ = 2048


def draw_decay_rates(key, part):
    slow_low = jnp.log(0.05 / SEQ)
    slow_high = jnp.log(2.0 / SEQ)
    slow_rates = jnp.exp(jax.random.uniform(jax.random.fold_in(key, 1), (HC, MODES), jnp.float32, slow_low, slow_high))
    fast_rates = jnp.exp(jax.random.uniform(jax.random.fold_in(key, 2), (HC, MODES), jnp.float32, jnp.log(0.02), jnp.log(0.05)))
    picker = jax.random.uniform(jax.random.fold_in(key, 3), (HC, MODES), jnp.float32)
    share = 0.5
    return jnp.where(picker < share, slow_rates, fast_rates).astype(jnp.float32)


def draw_queries(key, part):
    base = jnp.clip(jax.random.normal(jax.random.fold_in(key, 21), (SEQ, HA, HD), jnp.float32), -6.0, 6.0)
    return base.reshape(SEQ, HA * HD).astype(jnp.bfloat16)


def draw_key_vectors(key, part):
    base = jnp.clip(2.75 * jax.random.normal(jax.random.fold_in(key, 31), (SEQ, HA, HD), jnp.float32), -16.5, 16.5)
    return base.reshape(SEQ, HA * HD).astype(jnp.bfloat16)


def with_spikes(drawn, rng, source, target, parts, factor):
    def block_of(position):
        return (jnp.arange(drawn.shape[position]) // (drawn.shape[position] // parts)).reshape((-1,) + (1,) * (drawn.ndim - 1 - position))

    near = jax.random.permutation(rng, parts)[block_of(target)]
    far = (block_of(target) + parts // 2) % parts
    return jnp.where((block_of(source) == near) | (block_of(source) == far), factor * drawn, drawn)


def steps_of(key, shape, shards, low, high):
    def one(dim, parts):
        draws = jax.random.uniform(jax.random.fold_in(jax.random.fold_in(key, 6), dim), (parts,), jnp.float32, low / len(shards), high / len(shards))
        return jnp.repeat(jnp.exp(draws), shape[dim] // parts).reshape((-1,) + (1,) * (len(shape) - dim - 1))

    gain = one(*shards[0])
    for cut in shards[1:]:
        gain = gain * one(*cut)
    return gain


def centred(own_key, dims, spread, reach, pieces=(), kind=jnp.bfloat16):
    values = spread * jax.random.normal(own_key, dims, jnp.float32)
    if pieces:
        values = values * steps_of(own_key, dims, pieces, -0.22, 0.18)
    return jnp.clip(values, -reach, reach).astype(kind)


def bell_draw_with(key, extent, scale, most, pieces, heavy, kind=jnp.bfloat16):
    values = scale * jax.random.normal(key, extent, jnp.float32)
    if pieces:
        values = values * steps_of(key, extent, pieces, -0.22, 0.18)
    return jnp.clip(with_spikes(values, jax.random.fold_in(key, 3), *heavy), -most, most).astype(kind)


def setup_inputs(seed: int = 0) -> dict:
    splits = jax.random.split(jax.random.key(seed), 10)
    streams = centred(splits[0], (3, SEQ, HC), 1.0, 6.0, ((1, 8), (2, 4)))
    short_filter = centred(splits[1], (3, 7, HC), 7 ** -0.5, 2.0, ((2, 4),), jnp.float32)
    decay_rates = draw_decay_rates(jax.random.fold_in(splits[9], 71), 0)
    residues = centred(splits[3], (HC, MODES), 0.01, 0.06, ((0, 4),), jnp.float32)
    skip_gain = jnp.clip(0.5 + 1.0 * jax.random.uniform(splits[4], (HC,), jnp.float32) ** steps_of(splits[4], (HC,), ((0, 4),), -0.2, 0.2), 0.5, 1.5)
    hyena_weight = bell_draw_with(splits[5], (HC, D), HC ** -0.5, 0.1875, ((0, 4),), (0, 1, 4, 2.0))
    value_weight = bell_draw_with(splits[6], (D, HA * HD), D ** -0.5, 0.125, ((0, 4),), (0, 1, 4, 2.0))
    queries = draw_queries(jax.random.fold_in(splits[9], 71), 0)
    key_vectors = draw_key_vectors(jax.random.fold_in(splits[9], 71), 0)
    return dict(streams=streams, short_filter=short_filter, decay_rates=decay_rates, residues=residues, skip_gain=skip_gain, hyena_weight=hyena_weight, value_weight=value_weight, queries=queries, key_vectors=key_vectors)


def hyena_part(streams, short_filter, decay_rates, residues, skip_gain, hyena_weight):
    widened = streams.astype(jnp.float32)
    padded = jnp.pad(widened, ((0, 0), (6, 0), (0, 0)))
    filtered = jnp.zeros_like(widened)
    for offset in range(7):
        filtered = filtered + short_filter[:, offset, None, :] * padded[:, 6 - offset:6 - offset + SEQ, :]
    gate_part = filtered[0]
    product = filtered[1] * filtered[2]
    lags = jnp.arange(SEQ).astype(jnp.float32)
    kernel = jnp.zeros((SEQ, HC), jnp.float32)
    for mode in range(MODES):
        kernel = kernel + residues[:, mode][None, :] * jnp.exp(-decay_rates[:, mode][None, :] * lags[:, None])
    length = 2 * SEQ
    spectrum = jnp.fft.rfft(product, n=length, axis=0) * jnp.fft.rfft(kernel, n=length, axis=0)
    longconv = jnp.fft.irfft(spectrum, n=length, axis=0)[:SEQ]
    gated = (gate_part * (longconv + skip_gain[None, :] * product)).astype(jnp.bfloat16)
    return jnp.dot(gated, hyena_weight, preferred_element_type=jnp.float32).astype(jnp.bfloat16)

def attention_part(queries, key_vectors, values):
    block_rows = math.gcd(SEQ, 1024)
    block_count = SEQ // block_rows
    scale = 1.0 / math.sqrt(HD)
    query_heads = queries.reshape(SEQ, HA, HD).transpose(1, 0, 2)
    key_heads = key_vectors.reshape(SEQ, HA, HD).transpose(1, 0, 2)
    value_heads = values.reshape(SEQ, HA, HD).transpose(1, 0, 2)
    key_index = jnp.arange(SEQ).astype(jnp.int32)

    def one_block(index):
        head = (index // block_count).astype(jnp.int32)
        first = (index % block_count * block_rows).astype(jnp.int32)
        query_block = lax.dynamic_slice(query_heads, (head, first, jnp.int32(0)), (1, block_rows, HD))[0]
        key_head = lax.dynamic_index_in_dim(key_heads, head, 0, keepdims=False)
        value_head = lax.dynamic_index_in_dim(value_heads, head, 0, keepdims=False)
        scores = jnp.dot(query_block, key_head.T, preferred_element_type=jnp.float32) * scale
        query_index = first + jnp.arange(block_rows).astype(jnp.int32)
        allowed = key_index[None, :] <= query_index[:, None]
        top = lax.optimization_barrier(jnp.max(jnp.where(allowed, scores, -jnp.inf), axis=1))
        weights = jnp.where(allowed, jnp.exp(scores - top[:, None]), 0.0)
        total = lax.optimization_barrier(jnp.sum(weights, axis=1))
        summed = jnp.dot(weights.astype(jnp.bfloat16), value_head, preferred_element_type=jnp.float32)
        return (summed / total[:, None]).astype(jnp.bfloat16)
    blocks = lax.map(one_block, jnp.arange(HA * block_count).astype(jnp.int32))
    return blocks.reshape(HA, SEQ, HD).transpose(1, 0, 2).reshape(SEQ, HA * HD)

def reference(streams, short_filter, decay_rates, residues, skip_gain, hyena_weight, value_weight, queries, key_vectors):
    hyena_out = hyena_part(streams, short_filter, decay_rates, residues, skip_gain, hyena_weight)
    values = jnp.dot(hyena_out, value_weight, preferred_element_type=jnp.float32).astype(jnp.bfloat16)
    context = attention_part(queries, key_vectors, values)
    return (hyena_out, context)
```

```python
import functools
import math

import jax
import jax.numpy as jnp
from jax import lax
from jax.experimental import pallas as pl
from jax.experimental.pallas import tpu as pltpu
from jax.sharding import PartitionSpec as P

HD = 128
LANES = 128
SEGS = 8
HALO = 16
HALVES = 2
MESH = pl.DeviceIdType.MESH


def remote(source, target, send, recv, device):
    return pltpu.make_async_remote_copy(
        src_ref=source,
        dst_ref=target,
        send_sem=send,
        recv_sem=recv,
        device_id=device,
        device_id_type=MESH,
    )


class Grid:
    def __init__(self, ctx, me):
        self.side = math.isqrt(ctx // 2)
        assert 2 * self.side * self.side == ctx
        self.me = me
        self.chip, self.core = lax.div(me, 2), lax.rem(me, 2)
        self.a, self.b = lax.div(self.chip, self.side), lax.rem(self.chip, self.side)

    def at(self, first, second):
        da = first * self.core + second * (1 - self.core)
        db = second * self.core + first * (1 - self.core)
        chip = lax.rem(self.a + da, self.side) * self.side + lax.rem(self.b + db, self.side)
        return 2 * chip + self.core

    def sibling(self):
        return 2 * self.chip + 1 - self.core


class Gather:
    def __init__(self, grid, block, send, recv):
        self.grid, self.block, self.send, self.recv = grid, block, send, recv
        self.sent = []

    def push(self, owner, target):
        copy = remote(
            self.block(owner), self.block(owner), self.send(len(self.sent)), self.recv(owner), {"ctx": target}
        )
        copy.start()
        self.sent.append(copy)

    def wait(self, owner):
        remote(
            self.block(owner), self.block(owner), self.send(0), self.recv(owner), {"ctx": self.grid.sibling()}
        ).wait_recv()

    def own(self):
        grid = self.grid
        for k in range(1, grid.side):
            self.push(grid.me, grid.at(k, 0))
            self.push(grid.me, grid.at(0, k))
        self.push(grid.me, grid.sibling())

    def relay_first(self):
        grid = self.grid
        for k in range(1, grid.side):
            owner = grid.at(k, 0)
            self.wait(owner)
            for j in range(1, grid.side):
                self.push(owner, grid.at(0, j))
            self.push(owner, grid.sibling())

    def relay_second(self):
        grid = self.grid
        for j in range(1, grid.side):
            owner = grid.at(0, j)
            self.wait(owner)
            self.push(owner, grid.sibling())
        for j in range(1, grid.side):
            for k in range(1, grid.side):
                owner = grid.at(k, j)
                self.wait(owner)
                self.push(owner, grid.sibling())

    def take(self):
        grid = self.grid
        self.wait(grid.sibling())
        for j in range(grid.side):
            for k in range(grid.side):
                if j or k:
                    self.wait(grid.at(k, j) + 1 - 2 * grid.core)

    def finish(self):
        for copy in self.sent:
            copy.wait_send()


def sends_of(ctx):
    return ctx - 1


def body(
    ctx,
    tp,
    streams_hbm,
    taps_hbm,
    rates_hbm,
    res_hbm,
    skip_hbm,
    w_hbm,
    v_hbm,
    q_hbm,
    k_hbm,
    hyena_ref,
    out_ref,
    streams,
    prev,
    taps,
    rates_ref,
    residues,
    skips,
    ext,
    gate,
    u,
    seg,
    first,
    ends,
    gat,
    wfull,
    vv,
    q_ref,
    keys,
    vals,
    hacc,
    own_terms,
    snd,
    from_left,
    from_right,
    scores,
    probs,
    tops,
    totals,
    loc_sems,
    halo_sems,
    end_sems,
    wz_sems,
    wx_send,
    wx_recv,
    key_send,
    key_recv,
    val_send,
    val_recv,
    gat_send,
    gat_recv,
    sum_send,
    sum_recv,
):
    rows, width = q_ref.shape
    chans = streams.shape[2]
    blocks = chans // LANES
    half = rows // HALVES
    heads = width // HD
    modes = rates_ref.shape[0]
    steps = rows // SEGS
    wide = wfull.shape[3]
    f32 = jnp.float32
    me, z = lax.axis_index("ctx"), lax.axis_index("tp")
    grid = Grid(ctx, me)

    loads = [
        pltpu.make_async_copy(streams_hbm, streams, loc_sems.at[0]),
        pltpu.make_async_copy(taps_hbm, taps, loc_sems.at[1]),
        pltpu.make_async_copy(rates_hbm, rates_ref, loc_sems.at[2]),
        pltpu.make_async_copy(res_hbm, residues, loc_sems.at[3]),
        pltpu.make_async_copy(skip_hbm, skips, loc_sems.at[4]),
        pltpu.make_async_copy(k_hbm, keys.at[me], loc_sems.at[5]),
        pltpu.make_async_copy(q_hbm, q_ref, loc_sems.at[6]),
        pltpu.make_async_copy(
            w_hbm.at[:, :, pl.ds(pl.multiple_of(z * wide, wide), wide)], wfull.at[z], loc_sems.at[7]
        ),
    ] + [
        pltpu.make_async_copy(v_hbm.at[:, pl.ds(d * width, width)], vv.at[d], loc_sems.at[8 + d])
        for d in range(tp)
    ]
    for load in loads[:7]:
        load.start()

    barrier = pltpu.get_barrier_semaphore()
    for away in range(1, ctx):
        pl.semaphore_signal(barrier, inc=1, device_id={"ctx": lax.rem(me + away, ctx)}, device_id_type=MESH)
    for away in range(1, tp):
        pl.semaphore_signal(barrier, inc=1, device_id={"tp": lax.rem(z + away, tp)}, device_id_type=MESH)
    pl.semaphore_wait(barrier, tp - 1 + ctx - 1)

    halo = remote(
        streams_hbm.at[:, pl.ds(rows - HALO, HALO), :],
        prev,
        halo_sems.at[0],
        halo_sems.at[1],
        {"ctx": jnp.minimum(me + 1, ctx - 1)},
    )

    @pl.when(me < ctx - 1)
    def _():
        halo.start()

    shorter = jnp.minimum(z, tp - 1 - z)
    longer_way = jnp.where(z < tp - 1 - z, 1, -1)

    def near(j):
        paired = z + (j // 2 + 1) * (1 if j % 2 else -1)
        return jnp.where(j < 2 * shorter, paired, z + (j - shorter + 1) * longer_way)

    def w_copy(j):
        other = near(j)
        return remote(
            w_hbm.at[me, :, pl.ds(pl.multiple_of(other * wide, wide), wide)],
            wfull.at[z, me],
            wz_sems.at[0, j],
            wz_sems.at[1, z],
            {"tp": other},
        )

    def w_wait(j):
        source = near(j)
        remote(
            w_hbm.at[me, :, pl.ds(0, wide)], wfull.at[source, me], wz_sems.at[0, j], wz_sems.at[1, source], {"tp": source}
        ).wait_recv()

    def w_gather(j):
        source = near(j)
        return Gather(
            grid,
            lambda o: wfull.at[source, o],
            lambda i: wx_send.at[j, i],
            lambda o: wx_recv.at[j, o],
        )

    others = range(tp - 1)
    hops = range(1, tp)
    w_parts = [w_gather(j) for j in others]
    for j in others:
        w_copy(j).start()
    for load in loads[7:]:
        load.start()

    key_part = Gather(grid, lambda o: keys.at[o], lambda i: key_send.at[i], lambda o: key_recv.at[o])

    def val_gather(h):
        return Gather(
            grid, lambda o: vals.at[o, h], lambda i: val_send.at[h, i], lambda o: val_recv.at[h, o]
        )

    val_parts = [val_gather(h) for h in range(HALVES)]

    for load in loads[:5]:
        load.wait()

    @pl.when(me == 0)
    def _():
        prev[...] = jnp.zeros_like(prev)

    @pl.when(me > 0)
    def _():
        halo.wait_recv()

    def lanes_of(i):
        return pl.ds(pl.multiple_of(i * LANES, LANES), LANES)

    def pole_rows(value, n):
        return jnp.broadcast_to(value[n : n + 1], (SEGS, LANES))

    def filter_block(i, unused):
        at = lanes_of(i)
        outs = []
        for s in range(3):
            ext[s, :HALO, :] = prev[s, :, at].astype(f32)
            ext[s, HALO:, :] = streams[s, :, at].astype(f32)
        for s in range(3):
            tap = taps[s, :, at]
            acc = tap[0:1] * ext[s, HALO:, :]
            for j in range(1, 7):
                acc = acc + tap[j : j + 1] * ext[s, HALO - j : HALO - j + rows, :]
            outs.append(acc)
        gate[i] = outs[0]
        u[i] = outs[1] * outs[2]
        rates = rates_ref[:, at]
        decay = jnp.exp(-rates)
        factor = [pole_rows(decay, n) for n in range(modes)]
        state = [jnp.zeros((SEGS, LANES), f32) for _ in range(modes)]
        for step in range(steps):
            here = u[i, pl.ds(step, SEGS, stride=steps), :]
            for n in range(modes):
                state[n] = state[n] * factor[n] + here
        left = (steps * (SEGS - 1 - lax.broadcasted_iota(jnp.int32, (SEGS, LANES), 0))).astype(f32)
        for n in range(modes):
            seg[i, n * SEGS : (n + 1) * SEGS, :] = state[n]
            reach = jnp.exp(-pole_rows(rates, n) * left)
            ends[me, i, n : n + 1, :] = jnp.sum(reach * state[n], axis=0, keepdims=True)
        return unused

    lax.fori_loop(0, blocks, filter_block, 0)

    def end_copy(away):
        return remote(
            ends.at[me],
            ends.at[me],
            end_sems.at[0, away],
            end_sems.at[1, me],
            {"ctx": jnp.minimum(me + away, ctx - 1)},
        )

    def end_wait(o):
        remote(ends.at[o], ends.at[o], end_sems.at[0, 0], end_sems.at[1, o], {"ctx": grid.sibling()}).wait_recv()

    def each(count, act):
        def step(i, unused):
            act(i)
            return unused

        lax.fori_loop(0, count, step, 0)

    each(ctx - 1 - me, lambda i: end_copy(i + 1).start())
    w_wait(0)
    w_parts[0].own()
    each(me, end_wait)

    def mix_block(i, unused):
        at = lanes_of(i)
        rates = rates_ref[:, at]
        decay = jnp.exp(-rates)
        slab = jnp.exp(-rates * rows)
        hop = jnp.exp(-rates * steps)
        carried = lax.fori_loop(0, me, lambda o, c: c * slab + ends[o, i], jnp.zeros((modes, LANES), f32))
        for s in range(SEGS):
            first[pl.ds(s, modes, stride=SEGS), :] = carried
            carried = carried * hop + seg[i, pl.ds(s, modes, stride=SEGS), :]
        residue = residues[:, at]
        skip = jnp.broadcast_to(skips[:, at], (SEGS, LANES))
        factor = [pole_rows(decay, n) for n in range(modes)]
        weight = [pole_rows(residue, n) for n in range(modes)]
        state = [first[n * SEGS : (n + 1) * SEGS, :] for n in range(modes)]
        for step in range(steps):
            where = pl.ds(step, SEGS, stride=steps)
            here = u[i, where, :]
            terms = [skip * here, None]
            for n in range(modes):
                state[n] = state[n] * factor[n] + here
                term = weight[n] * state[n]
                terms[n % 2] = term if terms[n % 2] is None else terms[n % 2] + term
            gate[i, where, :] = gate[i, where, :] * (terms[0] + terms[1])
        for h in range(HALVES):
            gat[z, h, :, at] = gate[i, h * half : (h + 1) * half, :].astype(jnp.bfloat16)
        return unused

    lax.fori_loop(0, blocks, mix_block, 0)

    def gat_copy(source, h, way):
        return remote(
            gat.at[source, h],
            gat.at[source, h],
            gat_send.at[h, way, source],
            gat_recv.at[h, source],
            {"tp": jnp.clip(z + 1 - 2 * way, 0, tp - 1)},
        )

    def gat_give(source, h, way):
        @pl.when((z < tp - 1) if way == 0 else (z > 0))
        def _():
            gat_copy(source, h, way).start()

    def gat_own(h):
        for way in range(2):
            gat_give(z, h, way)

    def project(source, h, start):
        term = jnp.dot(
            gat[source, h], wfull[source].reshape(chans, wide), preferred_element_type=f32
        )
        if start:
            hacc[...] = term
        else:
            hacc[...] += term

    def gat_step(h, j):
        source = near(j)
        gat_copy(source, h, 0).wait_recv()

        @pl.when((source < z) & (z < tp - 1))
        def _():
            gat_copy(source, h, 0).start()

        @pl.when((source > z) & (z > 0))
        def _():
            gat_copy(source, h, 1).start()

    def all_terms(h):
        hyena = hacc[...].astype(jnp.bfloat16)
        hyena_ref[h * half : (h + 1) * half, :] = hyena
        for d in range(tp):
            own_terms[d] = jnp.dot(
                hyena_ref[h * half : (h + 1) * half, :], vv[d], preferred_element_type=f32
            )

    def sum_copy(d, h, way):
        box = from_left if way == 0 else from_right
        return remote(
            snd.at[h, d],
            box.at[h, d],
            sum_send.at[h, d],
            sum_recv.at[h, way, d],
            {"tp": jnp.clip(z + 1 - 2 * way, 0, tp - 1)},
        )

    def sum_step(h, k):
        for way in range(2):
            d = z + k if way == 0 else z - k

            @pl.when((d < tp) if way == 0 else (d >= 0))
            def _():
                box = from_left if way == 0 else from_right

                @pl.when((z > 0) if way == 0 else (z < tp - 1))
                def _():
                    sum_copy(d, h, way).wait_recv()
                    own_terms[d] += box[h, d].astype(f32)

                snd[h, d] = own_terms[d].astype(jnp.bfloat16)
                sum_copy(d, h, way).start()

    def sum_last(h):
        for way in range(2):
            box = from_left if way == 0 else from_right

            @pl.when((z > 0) if way == 0 else (z < tp - 1))
            def _():
                sum_copy(z, h, way).wait_recv()
                own_terms[z] += box[h, z].astype(f32)

        vals[me, h] = own_terms[z].astype(jnp.bfloat16)
        val_parts[h].own()

    scale = math.log2(math.e) / math.sqrt(HD)

    def weigh(head):
        here = slice(head * HD, (head + 1) * HD)

        def score(b):
            return (
                lax.dot_general(
                    q_ref[:, here], keys[b, :, here], (((1,), (1,)), ((), ())), preferred_element_type=f32
                )
                * scale
            )

        def fold(value, act):
            part = value[:, :HD]
            for at in range(HD, rows, HD):
                part = act(part, value[:, at : at + HD])
            return part

        query = lax.broadcasted_iota(jnp.int32, (rows, rows), 0)
        key = lax.broadcasted_iota(jnp.int32, (rows, rows), 1)
        mine = jnp.where(key <= query, score(me), -1e30)
        scores[me] = mine
        tops[...] = fold(mine, jnp.maximum)

        def earlier(b):
            value = score(b)
            scores[b] = value
            tops[...] = jnp.maximum(tops[...], fold(value, jnp.maximum))

        each(me, earlier)
        top = jnp.max(tops[...], axis=1, keepdims=True)
        tops[...] = jnp.broadcast_to(top, tops.shape)
        totals[head] = jnp.zeros_like(tops)

        def weight(b):
            value = jnp.exp2(scores[b] - tops[:, 0:1])
            totals[head] += fold(value, jnp.add)
            probs[head, b] = value.astype(jnp.bfloat16)

        each(me + 1, weight)
        totals[head] = jnp.broadcast_to(jnp.sum(totals[head], axis=1, keepdims=True), tops.shape)

    def blend(head):
        here = slice(head * HD, (head + 1) * HD)

        def step(b, acc):
            return acc + jnp.dot(
                probs[head, b], vals[b, :, :, here].reshape(rows, HD), preferred_element_type=f32
            )

        acc = lax.fori_loop(0, me + 1, step, jnp.zeros((rows, HD), f32))
        out_ref[:, here] = (acc / totals[head]).astype(jnp.bfloat16)

    loads[5].wait()
    gat_own(0)
    gat_own(1)
    w_wait(1)
    w_parts[1].own()
    w_parts[0].relay_first()
    for j in others[2:]:
        w_wait(j)
        w_parts[j].own()
    for j in others[1:]:
        w_parts[j].relay_first()
    gat_step(0, 0)
    key_part.own()
    for j in others:
        w_parts[j].relay_second()
    for load in loads[6:]:
        load.wait()
    project(z, 0, True)
    for j in others[1:]:
        gat_step(0, j)
    for j in others:
        w_parts[j].take()
        project(near(j), 0, False)
    all_terms(0)
    gat_step(1, 0)
    sum_step(0, tp - 1)
    key_part.relay_first()
    for j in others[1:]:
        gat_step(1, j)
        sum_step(0, tp - 1 - j)
    key_part.relay_second()
    project(z, 1, True)
    for j in others:
        project(near(j), 1, False)
    sum_last(0)
    all_terms(1)
    for k in reversed(hops):
        sum_step(1, k)
        if k == tp - 1:
            val_parts[0].relay_first()
            key_part.take()
    val_parts[0].relay_second()
    val_parts[0].take()
    for head in range(heads):
        weigh(head)
    sum_last(1)
    val_parts[1].relay_first()
    val_parts[1].relay_second()
    val_parts[1].take()
    for head in range(heads):
        blend(head)

    @pl.when(me < ctx - 1)
    def _():
        halo.wait_send()

    each(ctx - 1 - me, lambda i: end_copy(i + 1).wait_send())
    for j in others:
        w_copy(j).wait_send()
        w_parts[j].finish()
    key_part.finish()
    for h in range(HALVES):
        val_parts[h].finish()
        for way in range(2):

            @pl.when((z < tp - 1) if way == 0 else (z > 0))
            def _():
                gat_copy(z, h, way).wait_send()

        for j in others:
            source = near(j)

            @pl.when((source < z) & (z < tp - 1))
            def _():
                gat_copy(source, h, 0).wait_send()

            @pl.when((source > z) & (z > 0))
            def _():
                gat_copy(source, h, 1).wait_send()

        for k in hops:
            for way in range(2):
                d = z + k if way == 0 else z - k

                @pl.when((d < tp) if way == 0 else (d >= 0))
                def _():
                    sum_copy(d, h, way).wait_send()


def shards(streams, short_filter, decay_rates, residues, skip_gain, hyena_weight, value_weight, queries, key_vectors):
    ctx, tp = lax.axis_size("ctx"), lax.axis_size("tp")
    rows, chans = streams.shape[1:]
    width = queries.shape[1]
    wide = hyena_weight.shape[1] // tp
    deep = value_weight.shape[0]
    part = chans // ctx
    modes = decay_rates.shape[1]
    taps = short_filter.shape[1]
    blocks = chans // LANES
    heads = width // HD
    half = rows // HALVES
    f32, bf16 = jnp.float32, jnp.bfloat16
    dma = pltpu.SemaphoreType.DMA
    vmem = pltpu.VMEM
    return pl.pallas_call(
        functools.partial(body, ctx, tp),
        in_specs=[pl.BlockSpec(memory_space=pltpu.HBM)] * 9,
        out_specs=[pl.BlockSpec(memory_space=pltpu.VMEM)] * 2,
        out_shape=[
            jax.ShapeDtypeStruct((rows, wide), bf16),
            jax.ShapeDtypeStruct((rows, width), bf16),
        ],
        scratch_shapes=[
            vmem((3, rows, chans), bf16),
            vmem((3, HALO, chans), bf16),
            vmem((3, taps, chans), f32),
            vmem((modes, chans), f32),
            vmem((modes, chans), f32),
            vmem((1, chans), f32),
            vmem((3, rows + HALO, LANES), f32),
            vmem((blocks, rows, LANES), f32),
            vmem((blocks, rows, LANES), f32),
            vmem((blocks, modes * SEGS, LANES), f32),
            vmem((modes * SEGS, LANES), f32),
            vmem((ctx, blocks, modes, LANES), f32),
            vmem((tp, HALVES, half, chans), bf16),
            vmem((tp, ctx, part, wide), bf16),
            vmem((tp, deep, width), bf16),
            vmem((rows, width), bf16),
            vmem((ctx, rows, width), bf16),
            vmem((ctx, HALVES, half, width), bf16),
            vmem((half, wide), f32),
            vmem((tp, half, width), f32),
            vmem((HALVES, tp, half, width), bf16),
            vmem((HALVES, tp, half, width), bf16),
            vmem((HALVES, tp, half, width), bf16),
            vmem((ctx, rows, rows), f32),
            vmem((heads, ctx, rows, rows), bf16),
            vmem((rows, HD), f32),
            vmem((heads, rows, HD), f32),
            dma((8 + tp,)),
            dma((2,)),
            dma((2, ctx)),
            dma((2, tp)),
            dma((tp, ctx)),
            dma((tp, ctx)),
            dma((ctx,)),
            dma((ctx,)),
            dma((HALVES, ctx)),
            dma((HALVES, ctx)),
            dma((HALVES, 2, tp)),
            dma((HALVES, tp)),
            dma((HALVES, tp)),
            dma((HALVES, 2, tp)),
        ],
        cost_estimate=pl.CostEstimate(
            flops=4 * rows * ctx * rows * width,
            bytes_accessed=4 * ctx * rows * width,
            transcendentals=0,
        ),
        compiler_params=pltpu.CompilerParams(
            vmem_limit_bytes=56 * 1024 * 1024, collective_id=0, has_side_effects=True
        ),
        name="hyena_attention",
    )(
        streams,
        short_filter,
        decay_rates.T,
        residues.T,
        skip_gain[None],
        hyena_weight.reshape(ctx, part, tp * wide),
        value_weight,
        queries,
        key_vectors,
    )


def solution(mesh):
    return jax.shard_map(
        shards,
        mesh=mesh,
        in_specs=(
            P(None, "ctx", "tp"),
            P(None, None, "tp"),
            P("tp", None),
            P("tp", None),
            P("tp"),
            P("tp", None),
            P("tp", None),
            P("ctx", "tp"),
            P("ctx", "tp"),
        ),
        out_specs=(P("ctx", "tp"), P("ctx", "tp")),
        check_vma=False,
    )
```

```python
import functools
import math

import jax
import jax.numpy as jnp
from jax import lax
from jax.experimental import pallas as pl
from jax.experimental.pallas import tpu as pltpu
from jax.sharding import PartitionSpec as P

HD = 128
LANES = 128
SEGS = 8
HALO = 16
HALVES = 2
GAT_CUTS = 1
W_CUTS = 2
SUM_CUTS = 1
MESH = pl.DeviceIdType.MESH


def remote(source, target, send, recv, device):
    return pltpu.make_async_remote_copy(
        src_ref=source,
        dst_ref=target,
        send_sem=send,
        recv_sem=recv,
        device_id=device,
        device_id_type=MESH,
    )


class Grid:
    def __init__(self, ctx, me):
        self.side = math.isqrt(ctx // 2)
        assert 2 * self.side * self.side == ctx
        self.me = me
        self.chip, self.core = lax.div(me, 2), lax.rem(me, 2)
        self.a, self.b = lax.div(self.chip, self.side), lax.rem(self.chip, self.side)

    def at(self, first, second):
        da = first * self.core + second * (1 - self.core)
        db = second * self.core + first * (1 - self.core)
        chip = lax.rem(self.a + da, self.side) * self.side + lax.rem(self.b + db, self.side)
        return 2 * chip + self.core

    def sibling(self):
        return 2 * self.chip + 1 - self.core


class Gather:
    def __init__(self, grid, block, send, recv):
        self.grid, self.block, self.send, self.recv = grid, block, send, recv
        self.sent = []

    def push(self, owner, target):
        copy = remote(
            self.block(owner), self.block(owner), self.send(len(self.sent)), self.recv(owner), {"ctx": target}
        )
        copy.start()
        self.sent.append(copy)

    def wait(self, owner):
        remote(
            self.block(owner), self.block(owner), self.send(0), self.recv(owner), {"ctx": self.grid.sibling()}
        ).wait_recv()

    def own(self):
        grid = self.grid
        for j in reversed(range(grid.side)):
            for k in reversed(range(grid.side)):
                if j or k:
                    self.push(grid.me, grid.at(k, j))
        self.push(grid.me, grid.sibling())

    def own_lines(self):
        grid = self.grid
        for k in range(1, grid.side):
            self.push(grid.me, grid.at(k, 0))
            self.push(grid.me, grid.at(0, k))
        self.push(grid.me, grid.sibling())

    def relay_first(self):
        grid = self.grid
        for k in range(1, grid.side):
            owner = grid.at(k, 0)
            self.wait(owner)
            for j in range(1, grid.side):
                self.push(owner, grid.at(0, j))
            self.push(owner, grid.sibling())

    def relay_second(self):
        grid = self.grid
        for j in range(1, grid.side):
            for k in range(grid.side):
                owner = grid.at(k, j)
                self.wait(owner)
                self.push(owner, grid.sibling())

    def relay(self):
        grid = self.grid
        for j in range(grid.side):
            for k in range(grid.side):
                if j or k:
                    owner = grid.at(k, j)
                    self.wait(owner)
                    self.push(owner, grid.sibling())

    def take(self):
        grid = self.grid
        self.wait(grid.sibling())
        for j in range(grid.side):
            for k in range(grid.side):
                if j or k:
                    self.wait(grid.at(k, j) + 1 - 2 * grid.core)

    def finish(self):
        for copy in self.sent:
            copy.wait_send()


def sends_of(ctx):
    return ctx - 1


def body(
    ctx,
    tp,
    streams_hbm,
    taps_hbm,
    rates_hbm,
    res_hbm,
    skip_hbm,
    w_hbm,
    v_hbm,
    q_hbm,
    k_hbm,
    hyena_ref,
    out_ref,
    streams,
    prev,
    taps,
    rates_ref,
    residues,
    skips,
    ext,
    gate,
    u,
    seg,
    first,
    ends,
    gat,
    wfull,
    vv,
    q_ref,
    keys,
    vals,
    hacc,
    own_terms,
    snd,
    boxes,
    scores,
    probs,
    tops,
    totals,
    loc_sems,
    halo_sems,
    end_sems,
    wz_sems,
    wx_send,
    wx_recv,
    key_send,
    key_recv,
    val_send,
    val_recv,
    gat_send,
    gat_recv,
    sum_send,
    sum_recv,
):
    rows, width = q_ref.shape
    chans = streams.shape[2]
    blocks = chans // LANES
    half = rows // HALVES
    heads = width // HD
    modes = rates_ref.shape[0]
    steps = rows // SEGS
    wide = wfull.shape[3]
    part = wfull.shape[2]
    w_cuts = W_CUTS if part % (16 * W_CUTS) == 0 else 1
    f32 = jnp.float32
    me, z = lax.axis_index("ctx"), lax.axis_index("tp")
    grid = Grid(ctx, me)

    loads = [
        pltpu.make_async_copy(streams_hbm, streams, loc_sems.at[0]),
        pltpu.make_async_copy(taps_hbm, taps, loc_sems.at[1]),
        pltpu.make_async_copy(rates_hbm, rates_ref, loc_sems.at[2]),
        pltpu.make_async_copy(res_hbm, residues, loc_sems.at[3]),
        pltpu.make_async_copy(skip_hbm, skips, loc_sems.at[4]),
        pltpu.make_async_copy(k_hbm, keys.at[me], loc_sems.at[5]),
        pltpu.make_async_copy(q_hbm, q_ref, loc_sems.at[6]),
        pltpu.make_async_copy(
            w_hbm.at[:, :, pl.ds(pl.multiple_of(z * wide, wide), wide)], wfull.at[z], loc_sems.at[7]
        ),
    ] + [
        pltpu.make_async_copy(v_hbm.at[:, pl.ds(d * width, width)], vv.at[d], loc_sems.at[8 + d])
        for d in range(tp)
    ]
    for load in loads[:7]:
        load.start()

    barrier = pltpu.get_barrier_semaphore()
    for away in range(1, ctx):
        pl.semaphore_signal(barrier, inc=1, device_id={"ctx": lax.rem(me + away, ctx)}, device_id_type=MESH)
    for away in range(1, tp):
        pl.semaphore_signal(barrier, inc=1, device_id={"tp": lax.rem(z + away, tp)}, device_id_type=MESH)
    pl.semaphore_wait(barrier, tp - 1 + ctx - 1)

    halo = remote(
        streams_hbm.at[:, pl.ds(rows - HALO, HALO), :],
        prev,
        halo_sems.at[0],
        halo_sems.at[1],
        {"ctx": jnp.minimum(me + 1, ctx - 1)},
    )

    @pl.when(me < ctx - 1)
    def _():
        halo.start()

    shorter = jnp.minimum(z, tp - 1 - z)
    longer_way = jnp.where(z < tp - 1 - z, 1, -1)

    def near(j):
        paired = z + (j // 2 + 1) * (1 if j % 2 else -1)
        return jnp.where(j < 2 * shorter, paired, z + (j - shorter + 1) * longer_way)

    def w_rows(r):
        return pl.ds(r * (part // w_cuts), part // w_cuts)

    def w_copy(j, r):
        other = near(j)
        return remote(
            w_hbm.at[me, w_rows(r), pl.ds(pl.multiple_of(other * wide, wide), wide)],
            wfull.at[z, me, w_rows(r), :],
            wz_sems.at[0, r, j],
            wz_sems.at[1, r, z],
            {"tp": other},
        )

    def w_gather(j, r):
        source = near(j)
        return Gather(
            grid,
            lambda o: wfull.at[source, o, w_rows(r), :],
            lambda i: wx_send.at[r, j, i],
            lambda o: wx_recv.at[r, j, o],
        )

    def w_own(j, lines):
        for r in range(w_cuts):
            source = near(j)
            remote(
                w_hbm.at[me, w_rows(r), pl.ds(0, wide)],
                wfull.at[source, me, w_rows(r), :],
                wz_sems.at[0, r, j],
                wz_sems.at[1, r, source],
                {"tp": source},
            ).wait_recv()
            if lines:
                w_parts[j][r].own_lines()
            else:
                w_parts[j][r].own()

    def w_each(j, act):
        for item in w_parts[j]:
            act(item)

    others = range(tp - 1)
    hops = range(1, tp)
    w_parts = [[w_gather(j, r) for r in range(w_cuts)] for j in others]
    for j in others:
        for r in range(w_cuts):
            w_copy(j, r).start()
    for load in loads[7:]:
        load.start()

    key_part = Gather(grid, lambda o: keys.at[o], lambda i: key_send.at[i], lambda o: key_recv.at[o])

    def val_gather(h):
        return Gather(
            grid, lambda o: vals.at[o, h], lambda i: val_send.at[h, i], lambda o: val_recv.at[h, o]
        )

    val_parts = [val_gather(h) for h in range(HALVES)]

    loads[5].wait()
    key_part.own_lines()

    for load in loads[:5]:
        load.wait()

    @pl.when(me == 0)
    def _():
        prev[...] = jnp.zeros_like(prev)

    @pl.when(me > 0)
    def _():
        halo.wait_recv()

    def lanes_of(i):
        return pl.ds(pl.multiple_of(i * LANES, LANES), LANES)

    def pole_rows(value, n):
        return jnp.broadcast_to(value[n : n + 1], (SEGS, LANES))

    def filter_block(i, unused):
        at = lanes_of(i)
        outs = []
        for s in range(3):
            ext[s, :HALO, :] = prev[s, :, at].astype(f32)
            ext[s, HALO:, :] = streams[s, :, at].astype(f32)
        for s in range(3):
            tap = taps[s, :, at]
            acc = tap[0:1] * ext[s, HALO:, :]
            for j in range(1, 7):
                acc = acc + tap[j : j + 1] * ext[s, HALO - j : HALO - j + rows, :]
            outs.append(acc)
        gate[i] = outs[0]
        u[i] = outs[1] * outs[2]
        rates = rates_ref[:, at]
        decay = jnp.exp(-rates)
        factor = [pole_rows(decay, n) for n in range(modes)]
        state = [jnp.zeros((SEGS, LANES), f32) for _ in range(modes)]
        for step in range(steps):
            here = u[i, pl.ds(step, SEGS, stride=steps), :]
            for n in range(modes):
                state[n] = state[n] * factor[n] + here
        left = (steps * (SEGS - 1 - lax.broadcasted_iota(jnp.int32, (SEGS, LANES), 0))).astype(f32)
        for n in range(modes):
            seg[i, n * SEGS : (n + 1) * SEGS, :] = state[n]
            reach = jnp.exp(-pole_rows(rates, n) * left)
            ends[me, i, n : n + 1, :] = jnp.sum(reach * state[n], axis=0, keepdims=True)
        return unused

    lax.fori_loop(0, blocks, filter_block, 0)

    def end_copy(away):
        return remote(
            ends.at[me],
            ends.at[me],
            end_sems.at[0, away],
            end_sems.at[1, me],
            {"ctx": jnp.minimum(me + away, ctx - 1)},
        )

    def end_wait(o):
        remote(ends.at[o], ends.at[o], end_sems.at[0, 0], end_sems.at[1, o], {"ctx": grid.sibling()}).wait_recv()

    def each(count, act):
        def step(i, unused):
            act(i)
            return unused

        lax.fori_loop(0, count, step, 0)

    each(ctx - 1 - me, lambda i: end_copy(i + 1).start())
    w_own(0, True)
    each(me, end_wait)

    def mix_block(i, unused):
        at = lanes_of(i)
        rates = rates_ref[:, at]
        decay = jnp.exp(-rates)
        slab = jnp.exp(-rates * rows)
        hop = jnp.exp(-rates * steps)
        carried = lax.fori_loop(0, me, lambda o, c: c * slab + ends[o, i], jnp.zeros((modes, LANES), f32))
        for s in range(SEGS):
            first[pl.ds(s, modes, stride=SEGS), :] = carried
            carried = carried * hop + seg[i, pl.ds(s, modes, stride=SEGS), :]
        residue = residues[:, at]
        skip = jnp.broadcast_to(skips[:, at], (SEGS, LANES))
        factor = [pole_rows(decay, n) for n in range(modes)]
        weight = [pole_rows(residue, n) for n in range(modes)]
        state = [first[n * SEGS : (n + 1) * SEGS, :] for n in range(modes)]
        for step in range(steps):
            where = pl.ds(step, SEGS, stride=steps)
            here = u[i, where, :]
            terms = [skip * here, None]
            for n in range(modes):
                state[n] = state[n] * factor[n] + here
                term = weight[n] * state[n]
                terms[n % 2] = term if terms[n % 2] is None else terms[n % 2] + term
            gate[i, where, :] = gate[i, where, :] * (terms[0] + terms[1])
        for h in range(HALVES):
            gat[z, h, :, at] = gate[i, h * half : (h + 1) * half, :].astype(jnp.bfloat16)
        return unused

    lax.fori_loop(0, blocks, mix_block, 0)

    def gat_copy(source, c, way, hop):
        tall = half // GAT_CUTS
        place = gat.at[source, c // GAT_CUTS, pl.ds(c % GAT_CUTS * tall, tall), :]
        return remote(
            place,
            place,
            gat_send.at[c, way, hop, source],
            gat_recv.at[c, source],
            {"tp": jnp.clip(z + (hop + 1) * (1 - 2 * way), 0, tp - 1)},
        )

    def place_of(way):
        return z if way == 0 else tp - 1 - z

    def gat_pass(source, c, way, here, act):
        p = place_of(way)

        @pl.when(here & (p % 2 == 0) & (p + 2 < tp))
        def _():
            act(gat_copy(source, c, way, 1))

        @pl.when(here & (((p % 2 == 0) | (source == z)) & (p + 1 < tp)))
        def _():
            act(gat_copy(source, c, way, 0))

    def gat_own(c, act=lambda copy: copy.start()):
        for way in range(2):
            gat_pass(z, c, way, z >= 0, act)

    def gat_more(c, j, act=lambda copy: copy.start()):
        source = near(j)
        gat_pass(source, c, 0, source < z, act)
        gat_pass(source, c, 1, source > z, act)

    def gat_step(c, j):
        gat_copy(near(j), c, 0, 0).wait_recv()
        gat_more(c, j)

    def project(source, h, start):
        term = jnp.dot(
            gat[source, h], wfull[source].reshape(chans, wide), preferred_element_type=f32
        )
        if start:
            hacc[...] = term
        else:
            hacc[...] += term

    def all_terms(h):
        hyena = hacc[...].astype(jnp.bfloat16)
        hyena_ref[h * half : (h + 1) * half, :] = hyena
        for d in range(tp):
            own_terms[h, d] = jnp.dot(
                hyena_ref[h * half : (h + 1) * half, :], vv[d], preferred_element_type=f32
            )

    def sum_rows(c):
        tall = half // SUM_CUTS
        return pl.ds(c % SUM_CUTS * tall, tall)

    def sum_copy(d, c, way, hop):
        h, at = c // SUM_CUTS, sum_rows(c)
        return remote(
            snd.at[h, d, at, :],
            boxes.at[way, hop - 1, h, d, at, :],
            sum_send.at[c, d],
            sum_recv.at[c, way, hop - 1, d],
            {"tp": jnp.clip(z + hop * (1 - 2 * way), 0, tp - 1)},
        )

    def sum_add(d, c, way, hop):
        h, at = c // SUM_CUTS, sum_rows(c)

        @pl.when(place_of(way) >= hop)
        def _():
            sum_copy(d, c, way, hop).wait_recv()
            own_terms[h, d, at, :] += boxes[way, hop - 1, h, d, at, :].astype(f32)

    def sum_hop(k, way):
        return jnp.where(place_of(way) % 2 == 1, min(k, 2), 1)

    def sum_step(c, k, odd):
        h, at = c // SUM_CUTS, sum_rows(c)
        for way in range(2):
            d = z + k * (1 - 2 * way)
            p = place_of(way)

            @pl.when((p + k < tp) & (p % 2 == odd))
            def _():
                if odd:
                    sum_add(d, c, way, 1)
                    if tp > 4:
                        sum_add(d, c, way, 2)
                snd[h, d, at, :] = own_terms[h, d, at, :].astype(jnp.bfloat16)
                sum_copy(d, c, way, sum_hop(k, way)).start()

    def sum_last(h):
        for c in range(h * SUM_CUTS, (h + 1) * SUM_CUTS):
            for way in range(2):
                sum_add(z, c, way, 1)

                @pl.when(place_of(way) % 2 == 1)
                def _():
                    sum_add(z, c, way, 2)

        vals[me, h] = own_terms[h, z].astype(jnp.bfloat16)
        val_parts[h].own()

    scale = math.log2(math.e) / math.sqrt(HD)

    def weigh(head):
        here = slice(head * HD, (head + 1) * HD)

        def score(b):
            return (
                lax.dot_general(
                    q_ref[:, here], keys[b, :, here], (((1,), (1,)), ((), ())), preferred_element_type=f32
                )
                * scale
            )

        def fold(value, act):
            part = value[:, :HD]
            for at in range(HD, rows, HD):
                part = act(part, value[:, at : at + HD])
            return part

        query = lax.broadcasted_iota(jnp.int32, (rows, rows), 0)
        key = lax.broadcasted_iota(jnp.int32, (rows, rows), 1)
        mine = jnp.where(key <= query, score(me), -1e30)
        scores[me] = mine
        tops[...] = fold(mine, jnp.maximum)

        def earlier(b):
            value = score(b)
            scores[b] = value
            tops[...] = jnp.maximum(tops[...], fold(value, jnp.maximum))

        each(me, earlier)
        top = jnp.max(tops[...], axis=1, keepdims=True)
        tops[...] = jnp.broadcast_to(top, tops.shape)
        totals[head] = jnp.zeros_like(tops)

        def weight(b):
            value = jnp.exp2(scores[b] - tops[:, 0:1])
            totals[head] += fold(value, jnp.add)
            probs[head, b] = value.astype(jnp.bfloat16)

        each(me + 1, weight)
        totals[head] = jnp.broadcast_to(jnp.sum(totals[head], axis=1, keepdims=True), tops.shape)

    def blend(head):
        here = slice(head * HD, (head + 1) * HD)

        def step(b, acc):
            return acc + jnp.dot(
                probs[head, b], vals[b, :, :, here].reshape(rows, HD), preferred_element_type=f32
            )

        acc = lax.fori_loop(0, me + 1, step, jnp.zeros((rows, HD), f32))
        out_ref[:, here] = (acc / totals[head]).astype(jnp.bfloat16)

    gat_own(0)
    key_part.relay_first()
    w_own(1, True)
    w_each(0, Gather.relay_first)
    key_part.relay_second()
    key_part.take()
    loads[6].wait()
    weigh(0)
    w_each(0, Gather.relay_second)
    w_each(1, Gather.relay_first)
    for load in loads[7:]:
        load.wait()
    project(z, 0, True)
    for j in others[2:]:
        w_own(j, False)
    gat_step(0, 0)
    gat_own(1)
    weigh(1)
    w_each(1, Gather.relay_second)
    w_each(0, Gather.take)
    project(near(0), 0, False)
    gat_step(0, 1)
    w_each(1, Gather.take)
    project(near(1), 0, False)
    for j in others[2:]:
        w_each(j, Gather.relay)
        gat_step(0, j)
        w_each(j, Gather.take)
        project(near(j), 0, False)
    all_terms(0)
    for k in reversed(hops):
        sum_step(0, k, 0)
    gat_step(1, 0)
    gat_step(1, 1)
    for head in range(2, heads):
        weigh(head)
    for k in reversed(hops):
        sum_step(0, k, 1)
    for j in others[2:]:
        gat_step(1, j)
    project(z, 1, True)
    for j in others:
        project(near(j), 1, False)
    all_terms(1)
    for k in reversed(hops):
        sum_step(1, k, 0)
    sum_last(0)
    for k in reversed(hops):
        sum_step(1, k, 1)
    val_parts[0].relay()
    sum_last(1)
    val_parts[0].take()
    val_parts[1].relay()
    val_parts[1].take()
    for head in range(heads):
        blend(head)

    @pl.when(me < ctx - 1)
    def _():
        halo.wait_send()

    each(ctx - 1 - me, lambda i: end_copy(i + 1).wait_send())
    for j in others:
        for r in range(w_cuts):
            w_copy(j, r).wait_send()
        w_each(j, Gather.finish)
    key_part.finish()
    for h in range(HALVES):
        val_parts[h].finish()
    for c in range(HALVES * GAT_CUTS):
        gat_own(c, lambda copy: copy.wait_send())
        for j in others:
            gat_more(c, j, lambda copy: copy.wait_send())
    for c in range(HALVES * SUM_CUTS):
        for k in hops:
            for way in range(2):

                @pl.when(place_of(way) + k < tp)
                def _():
                    sum_copy(z + k * (1 - 2 * way), c, way, 1).wait_send()


def shards(streams, short_filter, decay_rates, residues, skip_gain, hyena_weight, value_weight, queries, key_vectors):
    ctx, tp = lax.axis_size("ctx"), lax.axis_size("tp")
    rows, chans = streams.shape[1:]
    width = queries.shape[1]
    wide = hyena_weight.shape[1] // tp
    deep = value_weight.shape[0]
    part = chans // ctx
    modes = decay_rates.shape[1]
    taps = short_filter.shape[1]
    blocks = chans // LANES
    heads = width // HD
    half = rows // HALVES
    f32, bf16 = jnp.float32, jnp.bfloat16
    dma = pltpu.SemaphoreType.DMA
    vmem = pltpu.VMEM
    return pl.pallas_call(
        functools.partial(body, ctx, tp),
        in_specs=[pl.BlockSpec(memory_space=pltpu.HBM)] * 9,
        out_specs=[pl.BlockSpec(memory_space=pltpu.VMEM)] * 2,
        out_shape=[
            jax.ShapeDtypeStruct((rows, wide), bf16),
            jax.ShapeDtypeStruct((rows, width), bf16),
        ],
        scratch_shapes=[
            vmem((3, rows, chans), bf16),
            vmem((3, HALO, chans), bf16),
            vmem((3, taps, chans), f32),
            vmem((modes, chans), f32),
            vmem((modes, chans), f32),
            vmem((1, chans), f32),
            vmem((3, rows + HALO, LANES), f32),
            vmem((blocks, rows, LANES), f32),
            vmem((blocks, rows, LANES), f32),
            vmem((blocks, modes * SEGS, LANES), f32),
            vmem((modes * SEGS, LANES), f32),
            vmem((ctx, blocks, modes, LANES), f32),
            vmem((tp, HALVES, half, chans), bf16),
            vmem((tp, ctx, part, wide), bf16),
            vmem((tp, deep, width), bf16),
            vmem((rows, width), bf16),
            vmem((ctx, rows, width), bf16),
            vmem((ctx, HALVES, half, width), bf16),
            vmem((half, wide), f32),
            vmem((HALVES, tp, half, width), f32),
            vmem((HALVES, tp, half, width), bf16),
            vmem((2, 2, HALVES, tp, half, width), bf16),
            vmem((ctx, rows, rows), f32),
            vmem((heads, ctx, rows, rows), bf16),
            vmem((rows, HD), f32),
            vmem((heads, rows, HD), f32),
            dma((8 + tp,)),
            dma((2,)),
            dma((2, ctx)),
            dma((2, W_CUTS, tp)),
            dma((W_CUTS, tp, ctx)),
            dma((W_CUTS, tp, ctx)),
            dma((ctx,)),
            dma((ctx,)),
            dma((HALVES, ctx)),
            dma((HALVES, ctx)),
            dma((HALVES * GAT_CUTS, 2, 2, tp)),
            dma((HALVES * GAT_CUTS, tp)),
            dma((HALVES * SUM_CUTS, tp)),
            dma((HALVES * SUM_CUTS, 2, 2, tp)),
        ],
        cost_estimate=pl.CostEstimate(
            flops=4 * rows * ctx * rows * width,
            bytes_accessed=4 * ctx * rows * width,
            transcendentals=0,
        ),
        compiler_params=pltpu.CompilerParams(
            vmem_limit_bytes=56 * 1024 * 1024, collective_id=0, has_side_effects=True
        ),
        name="hyena_attention",
    )(
        streams,
        short_filter,
        decay_rates.T,
        residues.T,
        skip_gain[None],
        hyena_weight.reshape(ctx, part, tp * wide),
        value_weight,
        queries,
        key_vectors,
    )


def solution(mesh):
    return jax.shard_map(
        shards,
        mesh=mesh,
        in_specs=(
            P(None, "ctx", "tp"),
            P(None, None, "tp"),
            P("tp", None),
            P("tp", None),
            P("tp"),
            P("tp", None),
            P("tp", None),
            P("ctx", "tp"),
            P("ctx", "tp"),
        ),
        out_specs=(P("ctx", "tp"), P("ctx", "tp")),
        check_vma=False,
    )
```

```python
import functools
import math

import jax
import jax.numpy as jnp
from jax import lax
from jax.experimental import pallas as pl
from jax.experimental.pallas import tpu as pltpu
from jax.sharding import PartitionSpec as P

HD = 128
LANES = 128
SEGS = 8
HALO = 16
HALVES = 2
GAT_CUTS = 1
W_CUTS = 2
SUM_CUTS = 1
MESH = pl.DeviceIdType.MESH


def remote(source, target, send, recv, device):
    return pltpu.make_async_remote_copy(
        src_ref=source,
        dst_ref=target,
        send_sem=send,
        recv_sem=recv,
        device_id=device,
        device_id_type=MESH,
    )


class Grid:
    def __init__(self, ctx, me):
        self.side = math.isqrt(ctx // 2)
        assert 2 * self.side * self.side == ctx
        self.me = me
        self.chip, self.core = lax.div(me, 2), lax.rem(me, 2)
        self.a, self.b = lax.div(self.chip, self.side), lax.rem(self.chip, self.side)

    def at(self, first, second):
        da = first * self.core + second * (1 - self.core)
        db = second * self.core + first * (1 - self.core)
        chip = lax.rem(self.a + da, self.side) * self.side + lax.rem(self.b + db, self.side)
        return 2 * chip + self.core

    def sibling(self):
        return 2 * self.chip + 1 - self.core


class Gather:
    def __init__(self, grid, block, send, recv):
        self.grid, self.block, self.send, self.recv = grid, block, send, recv
        self.sent = []

    def push(self, owner, target):
        copy = remote(
            self.block(owner), self.block(owner), self.send(len(self.sent)), self.recv(owner), {"ctx": target}
        )
        copy.start()
        self.sent.append(copy)

    def wait(self, owner):
        remote(
            self.block(owner), self.block(owner), self.send(0), self.recv(owner), {"ctx": self.grid.sibling()}
        ).wait_recv()

    def own(self):
        grid = self.grid
        for j in reversed(range(grid.side)):
            for k in reversed(range(grid.side)):
                if j or k:
                    self.push(grid.me, grid.at(k, j))
        self.push(grid.me, grid.sibling())

    def own_lines(self):
        grid = self.grid
        for k in range(1, grid.side):
            self.push(grid.me, grid.at(k, 0))
            self.push(grid.me, grid.at(0, k))
        self.push(grid.me, grid.sibling())

    def relay_first(self):
        grid = self.grid
        for k in range(1, grid.side):
            owner = grid.at(k, 0)
            self.wait(owner)
            for j in range(1, grid.side):
                self.push(owner, grid.at(0, j))
            self.push(owner, grid.sibling())

    def relay_second(self):
        grid = self.grid
        for j in range(1, grid.side):
            for k in range(grid.side):
                owner = grid.at(k, j)
                self.wait(owner)
                self.push(owner, grid.sibling())

    def relay(self):
        grid = self.grid
        for j in range(grid.side):
            for k in range(grid.side):
                if j or k:
                    owner = grid.at(k, j)
                    self.wait(owner)
                    self.push(owner, grid.sibling())

    def take(self):
        grid = self.grid
        self.wait(grid.sibling())
        for j in range(grid.side):
            for k in range(grid.side):
                if j or k:
                    self.wait(grid.at(k, j) + 1 - 2 * grid.core)

    def finish(self):
        for copy in self.sent:
            copy.wait_send()


def sends_of(ctx):
    return ctx - 1


def body(
    ctx,
    tp,
    streams_hbm,
    taps_hbm,
    rates_hbm,
    res_hbm,
    skip_hbm,
    w_hbm,
    v_hbm,
    q_hbm,
    k_hbm,
    hyena_ref,
    out_ref,
    streams,
    prev,
    taps,
    rates_ref,
    residues,
    skips,
    ext,
    gate,
    u,
    seg,
    first,
    ends,
    gat,
    w_own_rows,
    wfull,
    vv,
    q_ref,
    keys,
    vals,
    hacc,
    own_terms,
    snd,
    boxes,
    scores,
    probs,
    tops,
    totals,
    loc_sems,
    halo_sems,
    end_sems,
    wz_sems,
    wx_send,
    wx_recv,
    key_send,
    key_recv,
    val_send,
    val_recv,
    gat_send,
    gat_recv,
    sum_send,
    sum_recv,
):
    rows, width = q_ref.shape
    chans = streams.shape[2]
    blocks = chans // LANES
    half = rows // HALVES
    heads = width // HD
    modes = rates_ref.shape[0]
    steps = rows // SEGS
    wide = wfull.shape[3]
    part = wfull.shape[2]
    w_cuts = W_CUTS if part % (16 * W_CUTS) == 0 else 1
    f32 = jnp.float32
    me, z = lax.axis_index("ctx"), lax.axis_index("tp")
    grid = Grid(ctx, me)

    loads = [
        pltpu.make_async_copy(streams_hbm, streams, loc_sems.at[0]),
        pltpu.make_async_copy(taps_hbm, taps, loc_sems.at[1]),
        pltpu.make_async_copy(rates_hbm, rates_ref, loc_sems.at[2]),
        pltpu.make_async_copy(res_hbm, residues, loc_sems.at[3]),
        pltpu.make_async_copy(skip_hbm, skips, loc_sems.at[4]),
        pltpu.make_async_copy(k_hbm, keys.at[me], loc_sems.at[5]),
        pltpu.make_async_copy(q_hbm, q_ref, loc_sems.at[6]),
        pltpu.make_async_copy(
            w_hbm.at[:, :, pl.ds(pl.multiple_of(z * wide, wide), wide)], wfull.at[z], loc_sems.at[7]
        ),
    ] + [
        pltpu.make_async_copy(v_hbm.at[:, pl.ds(d * width, width)], vv.at[d], loc_sems.at[8 + d])
        for d in range(tp)
    ]
    shares = [
        pltpu.make_async_copy(w_hbm.at[me, :, pl.ds(d * wide, wide)], w_own_rows.at[d], loc_sems.at[8 + tp + d])
        for d in range(tp)
    ]
    for load in shares + loads[:7]:
        load.start()

    barrier = pltpu.get_barrier_semaphore()
    for away in range(1, ctx):
        pl.semaphore_signal(barrier, inc=1, device_id={"ctx": lax.rem(me + away, ctx)}, device_id_type=MESH)
    for away in range(1, tp):
        pl.semaphore_signal(barrier, inc=1, device_id={"tp": lax.rem(z + away, tp)}, device_id_type=MESH)
    pl.semaphore_wait(barrier, tp - 1 + ctx - 1)

    halo = remote(
        streams_hbm.at[:, pl.ds(rows - HALO, HALO), :],
        prev,
        halo_sems.at[0],
        halo_sems.at[1],
        {"ctx": jnp.minimum(me + 1, ctx - 1)},
    )

    @pl.when(me < ctx - 1)
    def _():
        halo.start()

    shorter = jnp.minimum(z, tp - 1 - z)
    longer_way = jnp.where(z < tp - 1 - z, 1, -1)

    def near(j):
        paired = z + (j // 2 + 1) * (2 * (j % 2) - 1)
        return jnp.where(j < 2 * shorter, paired, z + (j - shorter + 1) * longer_way)

    def w_rows(r):
        return pl.ds(r * (part // w_cuts), part // w_cuts)

    def w_copy(j, r):
        other = near(j)
        return remote(
            w_own_rows.at[other, w_rows(r), :],
            wfull.at[z, me, w_rows(r), :],
            wz_sems.at[0, r, j],
            wz_sems.at[1, r, z],
            {"tp": other},
        )

    def w_gather(j, r):
        source = near(j)
        return Gather(
            grid,
            lambda o: wfull.at[source, o, w_rows(r), :],
            lambda i: wx_send.at[r, j, i],
            lambda o: wx_recv.at[r, j, o],
        )

    def w_own(j, lines):
        for r in range(w_cuts):
            source = near(j)
            remote(
                w_own_rows.at[source, w_rows(r), :],
                wfull.at[source, me, w_rows(r), :],
                wz_sems.at[0, r, j],
                wz_sems.at[1, r, source],
                {"tp": source},
            ).wait_recv()
            if lines:
                w_parts[j][r].own_lines()
            else:
                w_parts[j][r].own()

    def w_each(j, act):
        for item in w_parts[j]:
            act(item)

    others = range(tp - 1)
    hops = range(1, tp)
    for load in shares:
        load.wait()
    w_parts = [[w_gather(j, r) for r in range(w_cuts)] for j in others]
    for j in others:
        turn = jnp.where((shorter == 0) & (j > 0), tp - 1 - j, j)
        for r in range(w_cuts):
            w_copy(turn, r).start()
    for load in loads[7:]:
        load.start()

    key_part = Gather(grid, lambda o: keys.at[o], lambda i: key_send.at[i], lambda o: key_recv.at[o])

    def val_gather(h):
        return Gather(
            grid, lambda o: vals.at[o, h], lambda i: val_send.at[h, i], lambda o: val_recv.at[h, o]
        )

    val_parts = [val_gather(h) for h in range(HALVES)]

    loads[5].wait()
    key_part.own_lines()

    for load in loads[:5]:
        load.wait()

    @pl.when(me == 0)
    def _():
        prev[...] = jnp.zeros_like(prev)

    @pl.when(me > 0)
    def _():
        halo.wait_recv()

    def lanes_of(i):
        return pl.ds(pl.multiple_of(i * LANES, LANES), LANES)

    def pole_rows(value, n):
        return jnp.broadcast_to(value[n : n + 1], (SEGS, LANES))

    def filter_block(i, unused):
        at = lanes_of(i)
        outs = []
        for s in range(3):
            ext[s, :HALO, :] = prev[s, :, at].astype(f32)
            ext[s, HALO:, :] = streams[s, :, at].astype(f32)
        for s in range(3):
            tap = taps[s, :, at]
            acc = tap[0:1] * ext[s, HALO:, :]
            for j in range(1, 7):
                acc = acc + tap[j : j + 1] * ext[s, HALO - j : HALO - j + rows, :]
            outs.append(acc)
        gate[i] = outs[0]
        u[i] = outs[1] * outs[2]
        rates = rates_ref[:, at]
        decay = jnp.exp(-rates)
        factor = [pole_rows(decay, n) for n in range(modes)]
        state = [jnp.zeros((SEGS, LANES), f32) for _ in range(modes)]
        for step in range(steps):
            here = u[i, pl.ds(step, SEGS, stride=steps), :]
            for n in range(modes):
                state[n] = state[n] * factor[n] + here
        left = (steps * (SEGS - 1 - lax.broadcasted_iota(jnp.int32, (SEGS, LANES), 0))).astype(f32)
        for n in range(modes):
            seg[i, n * SEGS : (n + 1) * SEGS, :] = state[n]
            reach = jnp.exp(-pole_rows(rates, n) * left)
            ends[me, i, n : n + 1, :] = jnp.sum(reach * state[n], axis=0, keepdims=True)
        return unused

    lax.fori_loop(0, blocks, filter_block, 0)

    def end_copy(away):
        return remote(
            ends.at[me],
            ends.at[me],
            end_sems.at[0, away],
            end_sems.at[1, me],
            {"ctx": jnp.minimum(me + away, ctx - 1)},
        )

    def end_wait(o):
        remote(ends.at[o], ends.at[o], end_sems.at[0, 0], end_sems.at[1, o], {"ctx": grid.sibling()}).wait_recv()

    def each(count, act):
        def step(i, unused):
            act(i)
            return unused

        lax.fori_loop(0, count, step, 0)

    each(ctx - 1 - me, lambda i: end_copy(i + 1).start())
    w_own(0, True)
    each(me, end_wait)

    def mix_block(i, unused):
        at = lanes_of(i)
        rates = rates_ref[:, at]
        decay = jnp.exp(-rates)
        slab = jnp.exp(-rates * rows)
        hop = jnp.exp(-rates * steps)
        carried = lax.fori_loop(0, me, lambda o, c: c * slab + ends[o, i], jnp.zeros((modes, LANES), f32))
        for s in range(SEGS):
            first[pl.ds(s, modes, stride=SEGS), :] = carried
            carried = carried * hop + seg[i, pl.ds(s, modes, stride=SEGS), :]
        residue = residues[:, at]
        skip = jnp.broadcast_to(skips[:, at], (SEGS, LANES))
        factor = [pole_rows(decay, n) for n in range(modes)]
        weight = [pole_rows(residue, n) for n in range(modes)]
        state = [first[n * SEGS : (n + 1) * SEGS, :] for n in range(modes)]
        for step in range(steps):
            where = pl.ds(step, SEGS, stride=steps)
            here = u[i, where, :]
            terms = [skip * here, None]
            for n in range(modes):
                state[n] = state[n] * factor[n] + here
                term = weight[n] * state[n]
                terms[n % 2] = term if terms[n % 2] is None else terms[n % 2] + term
            gate[i, where, :] = gate[i, where, :] * (terms[0] + terms[1])
        for h in range(HALVES):
            gat[z, h, :, at] = gate[i, h * half : (h + 1) * half, :].astype(jnp.bfloat16)
        return unused

    lax.fori_loop(0, blocks, mix_block, 0)

    def gat_copy(source, c, way, hop):
        tall = half // GAT_CUTS
        place = gat.at[source, c // GAT_CUTS, pl.ds(c % GAT_CUTS * tall, tall), :]
        return remote(
            place,
            place,
            gat_send.at[c, way, hop, source],
            gat_recv.at[c, source],
            {"tp": jnp.clip(z + (hop + 1) * (1 - 2 * way), 0, tp - 1)},
        )

    def place_of(way):
        return z if way == 0 else tp - 1 - z

    def gat_pass(source, c, way, here, act):
        p = place_of(way)

        @pl.when(here & (p % 2 == 0) & (p + 2 < tp))
        def _():
            act(gat_copy(source, c, way, 1))

        @pl.when(here & (((p % 2 == 0) | (source == z)) & (p + 1 < tp)))
        def _():
            act(gat_copy(source, c, way, 0))

    def gat_own(c, act=lambda copy: copy.start()):
        for way in range(2):
            gat_pass(z, c, way, z >= 0, act)

    def gat_more(c, j, act=lambda copy: copy.start()):
        source = near(j)
        gat_pass(source, c, 0, source < z, act)
        gat_pass(source, c, 1, source > z, act)

    def gat_step(c, j):
        gat_copy(near(j), c, 0, 0).wait_recv()
        gat_more(c, j)

    def project(source, h, start):
        term = jnp.dot(
            gat[source, h], wfull[source].reshape(chans, wide), preferred_element_type=f32
        )
        if start:
            hacc[...] = term
        else:
            hacc[...] += term

    def all_terms(h):
        hyena = hacc[...].astype(jnp.bfloat16)
        hyena_ref[h * half : (h + 1) * half, :] = hyena
        for d in range(tp):
            own_terms[h, d] = jnp.dot(
                hyena_ref[h * half : (h + 1) * half, :], vv[d], preferred_element_type=f32
            )

    def sum_rows(c):
        tall = half // SUM_CUTS
        return pl.ds(c % SUM_CUTS * tall, tall)

    def sum_copy(d, c, way, hop):
        h, at = c // SUM_CUTS, sum_rows(c)
        return remote(
            snd.at[h, d, at, :],
            boxes.at[way, hop - 1, h, d, at, :],
            sum_send.at[c, d],
            sum_recv.at[c, way, hop - 1, d],
            {"tp": jnp.clip(z + hop * (1 - 2 * way), 0, tp - 1)},
        )

    def sum_add(d, c, way, hop):
        h, at = c // SUM_CUTS, sum_rows(c)

        @pl.when(place_of(way) >= hop)
        def _():
            sum_copy(d, c, way, hop).wait_recv()
            own_terms[h, d, at, :] += boxes[way, hop - 1, h, d, at, :].astype(f32)

    def sum_hop(k, way):
        return jnp.where(place_of(way) % 2 == 1, min(k, 2), 1)

    def sum_step(c, k, odd):
        h, at = c // SUM_CUTS, sum_rows(c)
        for way in range(2):
            d = z + k * (1 - 2 * way)
            p = place_of(way)

            @pl.when((p + k < tp) & (p % 2 == odd))
            def _():
                if odd:
                    sum_add(d, c, way, 1)
                    if tp > 4:
                        sum_add(d, c, way, 2)
                snd[h, d, at, :] = own_terms[h, d, at, :].astype(jnp.bfloat16)
                sum_copy(d, c, way, sum_hop(k, way)).start()

    def sum_last(h):
        for c in range(h * SUM_CUTS, (h + 1) * SUM_CUTS):
            for way in range(2):
                sum_add(z, c, way, 1)

                @pl.when(place_of(way) % 2 == 1)
                def _():
                    sum_add(z, c, way, 2)

        vals[me, h] = own_terms[h, z].astype(jnp.bfloat16)
        val_parts[h].own()

    scale = math.log2(math.e) / math.sqrt(HD)

    def weigh(head):
        here = slice(head * HD, (head + 1) * HD)

        def score(b):
            return (
                lax.dot_general(
                    q_ref[:, here], keys[b, :, here], (((1,), (1,)), ((), ())), preferred_element_type=f32
                )
                * scale
            )

        def fold(value, act):
            part = value[:, :HD]
            for at in range(HD, rows, HD):
                part = act(part, value[:, at : at + HD])
            return part

        query = lax.broadcasted_iota(jnp.int32, (rows, rows), 0)
        key = lax.broadcasted_iota(jnp.int32, (rows, rows), 1)
        mine = jnp.where(key <= query, score(me), -1e30)
        scores[me] = mine
        tops[...] = fold(mine, jnp.maximum)

        def earlier(b):
            value = score(b)
            scores[b] = value
            tops[...] = jnp.maximum(tops[...], fold(value, jnp.maximum))

        each(me, earlier)
        top = jnp.max(tops[...], axis=1, keepdims=True)
        tops[...] = jnp.broadcast_to(top, tops.shape)
        totals[head] = jnp.zeros_like(tops)

        def weight(b):
            value = jnp.exp2(scores[b] - tops[:, 0:1])
            totals[head] += fold(value, jnp.add)
            probs[head, b] = value.astype(jnp.bfloat16)

        each(me + 1, weight)
        totals[head] = jnp.broadcast_to(jnp.sum(totals[head], axis=1, keepdims=True), tops.shape)

    def blend(head):
        here = slice(head * HD, (head + 1) * HD)

        def step(b, acc):
            return acc + jnp.dot(
                probs[head, b], vals[b, :, :, here].reshape(rows, HD), preferred_element_type=f32
            )

        acc = lax.fori_loop(0, me + 1, step, jnp.zeros((rows, HD), f32))
        out_ref[:, here] = (acc / totals[head]).astype(jnp.bfloat16)

    gat_own(0)
    key_part.relay_first()
    w_own(1, True)
    w_each(0, Gather.relay_first)
    key_part.relay_second()
    key_part.take()
    loads[6].wait()
    weigh(0)
    w_each(0, Gather.relay_second)
    w_each(1, Gather.relay_first)
    for load in loads[7:]:
        load.wait()
    project(z, 0, True)
    for j in others[2:]:
        w_own(j, False)
    gat_step(0, 0)
    gat_own(1)
    weigh(1)
    w_each(1, Gather.relay_second)
    w_each(0, Gather.take)
    project(near(0), 0, False)
    gat_step(0, 1)
    w_each(1, Gather.take)
    project(near(1), 0, False)
    for j in others[2:]:
        w_each(j, Gather.relay)
        gat_step(0, j)
        w_each(j, Gather.take)
        project(near(j), 0, False)
    all_terms(0)
    for k in reversed(hops):
        sum_step(0, k, 0)
    gat_step(1, 0)
    gat_step(1, 1)
    weigh(2) if heads > 2 else None
    for k in reversed(hops):
        sum_step(0, k, 1)
    for j in others[2:]:
        gat_step(1, j)
    project(z, 1, True)
    for j in others:
        project(near(j), 1, False)
    all_terms(1)
    for k in reversed(hops):
        sum_step(1, k, 0)
    sum_last(0)
    for head in range(3, heads):
        weigh(head)
    for k in reversed(hops):
        sum_step(1, k, 1)
    val_parts[0].relay()
    sum_last(1)
    val_parts[0].take()
    val_parts[1].relay()
    val_parts[1].take()
    for head in range(heads):
        blend(head)

    @pl.when(me < ctx - 1)
    def _():
        halo.wait_send()

    each(ctx - 1 - me, lambda i: end_copy(i + 1).wait_send())
    for j in others:
        for r in range(w_cuts):
            w_copy(j, r).wait_send()
        w_each(j, Gather.finish)
    key_part.finish()
    for h in range(HALVES):
        val_parts[h].finish()
    for c in range(HALVES * GAT_CUTS):
        gat_own(c, lambda copy: copy.wait_send())
        for j in others:
            gat_more(c, j, lambda copy: copy.wait_send())
    for c in range(HALVES * SUM_CUTS):
        for k in hops:
            for way in range(2):

                @pl.when(place_of(way) + k < tp)
                def _():
                    sum_copy(z + k * (1 - 2 * way), c, way, 1).wait_send()


def shards(streams, short_filter, decay_rates, residues, skip_gain, hyena_weight, value_weight, queries, key_vectors):
    ctx, tp = lax.axis_size("ctx"), lax.axis_size("tp")
    rows, chans = streams.shape[1:]
    width = queries.shape[1]
    wide = hyena_weight.shape[1] // tp
    deep = value_weight.shape[0]
    part = chans // ctx
    modes = decay_rates.shape[1]
    taps = short_filter.shape[1]
    blocks = chans // LANES
    heads = width // HD
    half = rows // HALVES
    f32, bf16 = jnp.float32, jnp.bfloat16
    dma = pltpu.SemaphoreType.DMA
    vmem = pltpu.VMEM
    return pl.pallas_call(
        functools.partial(body, ctx, tp),
        in_specs=[pl.BlockSpec(memory_space=pltpu.HBM)] * 9,
        out_specs=[pl.BlockSpec(memory_space=pltpu.VMEM)] * 2,
        out_shape=[
            jax.ShapeDtypeStruct((rows, wide), bf16),
            jax.ShapeDtypeStruct((rows, width), bf16),
        ],
        scratch_shapes=[
            vmem((3, rows, chans), bf16),
            vmem((3, HALO, chans), bf16),
            vmem((3, taps, chans), f32),
            vmem((modes, chans), f32),
            vmem((modes, chans), f32),
            vmem((1, chans), f32),
            vmem((3, rows + HALO, LANES), f32),
            vmem((blocks, rows, LANES), f32),
            vmem((blocks, rows, LANES), f32),
            vmem((blocks, modes * SEGS, LANES), f32),
            vmem((modes * SEGS, LANES), f32),
            vmem((ctx, blocks, modes, LANES), f32),
            vmem((tp, HALVES, half, chans), bf16),
            vmem((tp, part, wide), bf16),
            vmem((tp, ctx, part, wide), bf16),
            vmem((tp, deep, width), bf16),
            vmem((rows, width), bf16),
            vmem((ctx, rows, width), bf16),
            vmem((ctx, HALVES, half, width), bf16),
            vmem((half, wide), f32),
            vmem((HALVES, tp, half, width), f32),
            vmem((HALVES, tp, half, width), bf16),
            vmem((2, 2, HALVES, tp, half, width), bf16),
            vmem((ctx, rows, rows), f32),
            vmem((heads, ctx, rows, rows), bf16),
            vmem((rows, HD), f32),
            vmem((heads, rows, HD), f32),
            dma((8 + 2 * tp,)),
            dma((2,)),
            dma((2, ctx)),
            dma((2, W_CUTS, tp)),
            dma((W_CUTS, tp, ctx)),
            dma((W_CUTS, tp, ctx)),
            dma((ctx,)),
            dma((ctx,)),
            dma((HALVES, ctx)),
            dma((HALVES, ctx)),
            dma((HALVES * GAT_CUTS, 2, 2, tp)),
            dma((HALVES * GAT_CUTS, tp)),
            dma((HALVES * SUM_CUTS, tp)),
            dma((HALVES * SUM_CUTS, 2, 2, tp)),
        ],
        cost_estimate=pl.CostEstimate(
            flops=4 * rows * ctx * rows * width,
            bytes_accessed=4 * ctx * rows * width,
            transcendentals=0,
        ),
        compiler_params=pltpu.CompilerParams(
            vmem_limit_bytes=56 * 1024 * 1024, collective_id=0, has_side_effects=True
        ),
        name="hyena_attention",
    )(
        streams,
        short_filter,
        decay_rates.T,
        residues.T,
        skip_gain[None],
        hyena_weight.reshape(ctx, part, tp * wide),
        value_weight,
        queries,
        key_vectors,
    )


def solution(mesh):
    return jax.shard_map(
        shards,
        mesh=mesh,
        in_specs=(
            P(None, "ctx", "tp"),
            P(None, None, "tp"),
            P("tp", None),
            P("tp", None),
            P("tp"),
            P("tp", None),
            P("tp", None),
            P("ctx", "tp"),
            P("ctx", "tp"),
        ),
        out_specs=(P("ctx", "tp"), P("ctx", "tp")),
        check_vma=False,
    )
```

```python
import functools
import math

import jax
import jax.numpy as jnp
from jax import lax
from jax.experimental import pallas as pl
from jax.experimental.pallas import tpu as pltpu
from jax.sharding import PartitionSpec as P

HD = 128
LANES = 128
SEGS = 8
HALO = 16
HALVES = 2
GAT_CUTS = 1
W_CUTS = 2
SUM_CUTS = 1
MESH = pl.DeviceIdType.MESH


def remote(source, target, send, recv, device):
    return pltpu.make_async_remote_copy(
        src_ref=source,
        dst_ref=target,
        send_sem=send,
        recv_sem=recv,
        device_id=device,
        device_id_type=MESH,
    )


class Grid:
    def __init__(self, ctx, me):
        self.side = math.isqrt(ctx // 2)
        assert 2 * self.side * self.side == ctx
        self.me = me
        self.chip, self.core = lax.div(me, 2), lax.rem(me, 2)
        self.a, self.b = lax.div(self.chip, self.side), lax.rem(self.chip, self.side)

    def at(self, first, second):
        da = first * self.core + second * (1 - self.core)
        db = second * self.core + first * (1 - self.core)
        chip = lax.rem(self.a + da, self.side) * self.side + lax.rem(self.b + db, self.side)
        return 2 * chip + self.core

    def sibling(self):
        return 2 * self.chip + 1 - self.core


class Gather:
    def __init__(self, grid, block, send, recv):
        self.grid, self.block, self.send, self.recv = grid, block, send, recv
        self.sent = []

    def push(self, owner, target):
        copy = remote(
            self.block(owner), self.block(owner), self.send(len(self.sent)), self.recv(owner), {"ctx": target}
        )
        copy.start()
        self.sent.append(copy)

    def wait(self, owner):
        remote(
            self.block(owner), self.block(owner), self.send(0), self.recv(owner), {"ctx": self.grid.sibling()}
        ).wait_recv()

    def own(self):
        grid = self.grid
        for j in reversed(range(grid.side)):
            for k in reversed(range(grid.side)):
                if j or k:
                    self.push(grid.me, grid.at(k, j))
        self.push(grid.me, grid.sibling())

    def own_lines(self):
        grid = self.grid
        for k in range(1, grid.side):
            self.push(grid.me, grid.at(k, 0))
            self.push(grid.me, grid.at(0, k))
        self.push(grid.me, grid.sibling())

    def relay_first(self):
        grid = self.grid
        for k in range(1, grid.side):
            owner = grid.at(k, 0)
            self.wait(owner)
            for j in range(1, grid.side):
                self.push(owner, grid.at(0, j))
            self.push(owner, grid.sibling())

    def relay_second(self):
        grid = self.grid
        for j in range(1, grid.side):
            for k in range(grid.side):
                owner = grid.at(k, j)
                self.wait(owner)
                self.push(owner, grid.sibling())

    def relay(self):
        grid = self.grid
        for j in range(grid.side):
            for k in range(grid.side):
                if j or k:
                    owner = grid.at(k, j)
                    self.wait(owner)
                    self.push(owner, grid.sibling())

    def take(self):
        grid = self.grid
        self.wait(grid.sibling())
        for j in range(grid.side):
            for k in range(grid.side):
                if j or k:
                    self.wait(grid.at(k, j) + 1 - 2 * grid.core)

    def finish(self):
        for copy in self.sent:
            copy.wait_send()


def sends_of(ctx):
    return ctx - 1


def body(
    ctx,
    tp,
    streams_hbm,
    taps_hbm,
    rates_hbm,
    res_hbm,
    skip_hbm,
    w_hbm,
    v_hbm,
    q_hbm,
    k_hbm,
    hyena_ref,
    out_ref,
    streams,
    prev,
    taps,
    rates_ref,
    residues,
    skips,
    ext,
    gate,
    u,
    seg,
    first,
    ends,
    gat,
    w_own_rows,
    wfull,
    vv,
    q_ref,
    keys,
    vals,
    hacc,
    own_terms,
    snd,
    boxes,
    scores,
    probs,
    tops,
    totals,
    loc_sems,
    halo_sems,
    end_sems,
    wz_sems,
    wx_send,
    wx_recv,
    key_send,
    key_recv,
    val_send,
    val_recv,
    gat_send,
    gat_recv,
    sum_send,
    sum_recv,
):
    rows, width = q_ref.shape
    chans = streams.shape[2]
    blocks = chans // LANES
    half = rows // HALVES
    heads = width // HD
    modes = rates_ref.shape[0]
    steps = rows // SEGS
    wide = wfull.shape[3]
    part = wfull.shape[2]
    w_cuts = W_CUTS if part % (16 * W_CUTS) == 0 else 1
    f32 = jnp.float32
    me, z = lax.axis_index("ctx"), lax.axis_index("tp")
    grid = Grid(ctx, me)

    loads = [
        pltpu.make_async_copy(streams_hbm, streams, loc_sems.at[0]),
        pltpu.make_async_copy(taps_hbm, taps, loc_sems.at[1]),
        pltpu.make_async_copy(rates_hbm, rates_ref, loc_sems.at[2]),
        pltpu.make_async_copy(res_hbm, residues, loc_sems.at[3]),
        pltpu.make_async_copy(skip_hbm, skips, loc_sems.at[4]),
        pltpu.make_async_copy(k_hbm, keys.at[me], loc_sems.at[5]),
        pltpu.make_async_copy(q_hbm, q_ref, loc_sems.at[6]),
        pltpu.make_async_copy(
            w_hbm.at[:, :, pl.ds(pl.multiple_of(z * wide, wide), wide)], wfull.at[z], loc_sems.at[7]
        ),
    ] + [
        pltpu.make_async_copy(v_hbm.at[:, pl.ds(d * width, width)], vv.at[d], loc_sems.at[8 + d])
        for d in range(tp)
    ]
    shares = [
        pltpu.make_async_copy(w_hbm.at[me, :, pl.ds(d * wide, wide)], w_own_rows.at[d], loc_sems.at[8 + tp + d])
        for d in range(tp)
    ]
    for load in shares + loads[:7]:
        load.start()

    barrier = pltpu.get_barrier_semaphore()
    for away in range(1, ctx):
        pl.semaphore_signal(barrier, inc=1, device_id={"ctx": lax.rem(me + away, ctx)}, device_id_type=MESH)
    for away in range(1, tp):
        pl.semaphore_signal(barrier, inc=1, device_id={"tp": lax.rem(z + away, tp)}, device_id_type=MESH)
    pl.semaphore_wait(barrier, tp - 1 + ctx - 1)

    halo = remote(
        streams_hbm.at[:, pl.ds(rows - HALO, HALO), :],
        prev,
        halo_sems.at[0],
        halo_sems.at[1],
        {"ctx": jnp.minimum(me + 1, ctx - 1)},
    )

    @pl.when(me < ctx - 1)
    def _():
        halo.start()

    shorter = jnp.minimum(z, tp - 1 - z)
    longer_way = jnp.where(z < tp - 1 - z, 1, -1)

    def near(j):
        paired = z + (j // 2 + 1) * (2 * (j % 2) - 1)
        return jnp.where(j < 2 * shorter, paired, z + (j - shorter + 1) * longer_way)

    def w_rows(r):
        return pl.ds(r * (part // w_cuts), part // w_cuts)

    def w_copy(j, r):
        other = near(j)
        return remote(
            w_own_rows.at[other, w_rows(r), :],
            wfull.at[z, me, w_rows(r), :],
            wz_sems.at[0, r, j],
            wz_sems.at[1, r, z],
            {"tp": other},
        )

    def w_gather(j, r):
        source = near(j)
        return Gather(
            grid,
            lambda o: wfull.at[source, o, w_rows(r), :],
            lambda i: wx_send.at[r, j, i],
            lambda o: wx_recv.at[r, j, o],
        )

    def w_own(j, lines):
        for r in range(w_cuts):
            source = near(j)
            remote(
                w_own_rows.at[source, w_rows(r), :],
                wfull.at[source, me, w_rows(r), :],
                wz_sems.at[0, r, j],
                wz_sems.at[1, r, source],
                {"tp": source},
            ).wait_recv()
            if lines:
                w_parts[j][r].own_lines()
            else:
                w_parts[j][r].own()

    def w_each(j, act):
        for item in w_parts[j]:
            act(item)

    others = range(tp - 1)
    hops = range(1, tp)
    for load in shares:
        load.wait()
    w_parts = [[w_gather(j, r) for r in range(w_cuts)] for j in others]
    for j in others:
        turn = jnp.where((shorter == 0) & (j > 0), tp - 1 - j, j)
        for r in range(w_cuts):
            w_copy(turn, r).start()
    for load in loads[7:]:
        load.start()

    key_part = Gather(grid, lambda o: keys.at[o], lambda i: key_send.at[i], lambda o: key_recv.at[o])

    def val_gather(h):
        return Gather(
            grid, lambda o: vals.at[o, h], lambda i: val_send.at[h, i], lambda o: val_recv.at[h, o]
        )

    val_parts = [val_gather(h) for h in range(HALVES)]

    loads[5].wait()
    key_part.own_lines()

    for load in loads[:5]:
        load.wait()

    @pl.when(me == 0)
    def _():
        prev[...] = jnp.zeros_like(prev)

    @pl.when(me > 0)
    def _():
        halo.wait_recv()

    def lanes_of(i):
        return pl.ds(pl.multiple_of(i * LANES, LANES), LANES)

    def pole_rows(value, n):
        return jnp.broadcast_to(value[n : n + 1], (SEGS, LANES))

    def filter_block(i, unused):
        at = lanes_of(i)
        outs = []
        for s in range(3):
            ext[s, :HALO, :] = prev[s, :, at].astype(f32)
            ext[s, HALO:, :] = streams[s, :, at].astype(f32)
        for s in range(3):
            tap = taps[s, :, at]
            acc = tap[0:1] * ext[s, HALO:, :]
            for j in range(1, 7):
                acc = acc + tap[j : j + 1] * ext[s, HALO - j : HALO - j + rows, :]
            outs.append(acc)
        gate[i] = outs[0]
        u[i] = outs[1] * outs[2]
        rates = rates_ref[:, at]
        decay = jnp.exp(-rates)
        factor = [pole_rows(decay, n) for n in range(modes)]
        state = [jnp.zeros((SEGS, LANES), f32) for _ in range(modes)]
        for step in range(steps):
            here = u[i, pl.ds(step, SEGS, stride=steps), :]
            for n in range(modes):
                state[n] = state[n] * factor[n] + here
        left = (steps * (SEGS - 1 - lax.broadcasted_iota(jnp.int32, (SEGS, LANES), 0))).astype(f32)
        for n in range(modes):
            seg[i, n * SEGS : (n + 1) * SEGS, :] = state[n]
            reach = jnp.exp(-pole_rows(rates, n) * left)
            ends[me, i, n : n + 1, :] = jnp.sum(reach * state[n], axis=0, keepdims=True)
        return unused

    lax.fori_loop(0, blocks, filter_block, 0)

    def end_copy(away):
        return remote(
            ends.at[me],
            ends.at[me],
            end_sems.at[0, away],
            end_sems.at[1, me],
            {"ctx": jnp.minimum(me + away, ctx - 1)},
        )

    def end_wait(o):
        remote(ends.at[o], ends.at[o], end_sems.at[0, 0], end_sems.at[1, o], {"ctx": grid.sibling()}).wait_recv()

    def each(count, act):
        def step(i, unused):
            act(i)
            return unused

        lax.fori_loop(0, count, step, 0)

    each(ctx - 1 - me, lambda i: end_copy(i + 1).start())
    w_own(0, True)
    each(me, end_wait)

    def mix_block(i, unused):
        at = lanes_of(i)
        rates = rates_ref[:, at]
        decay = jnp.exp(-rates)
        slab = jnp.exp(-rates * rows)
        hop = jnp.exp(-rates * steps)
        carried = lax.fori_loop(0, me, lambda o, c: c * slab + ends[o, i], jnp.zeros((modes, LANES), f32))
        for s in range(SEGS):
            first[pl.ds(s, modes, stride=SEGS), :] = carried
            carried = carried * hop + seg[i, pl.ds(s, modes, stride=SEGS), :]
        residue = residues[:, at]
        skip = jnp.broadcast_to(skips[:, at], (SEGS, LANES))
        factor = [pole_rows(decay, n) for n in range(modes)]
        weight = [pole_rows(residue, n) for n in range(modes)]
        state = [first[n * SEGS : (n + 1) * SEGS, :] for n in range(modes)]
        for step in range(steps):
            where = pl.ds(step, SEGS, stride=steps)
            here = u[i, where, :]
            terms = [skip * here, None]
            for n in range(modes):
                state[n] = state[n] * factor[n] + here
                term = weight[n] * state[n]
                terms[n % 2] = term if terms[n % 2] is None else terms[n % 2] + term
            gate[i, where, :] = gate[i, where, :] * (terms[0] + terms[1])
        for h in range(HALVES):
            gat[z, h, :, at] = gate[i, h * half : (h + 1) * half, :].astype(jnp.bfloat16)
        return unused

    lax.fori_loop(0, blocks, mix_block, 0)

    def gat_copy(source, c, way, hop):
        tall = half // GAT_CUTS
        place = gat.at[source, c // GAT_CUTS, pl.ds(c % GAT_CUTS * tall, tall), :]
        return remote(
            place,
            place,
            gat_send.at[c, way, hop, source],
            gat_recv.at[c, source],
            {"tp": jnp.clip(z + (hop + 1) * (1 - 2 * way), 0, tp - 1)},
        )

    def place_of(way):
        return z if way == 0 else tp - 1 - z

    def gat_pass(source, c, way, here, act):
        p = place_of(way)

        @pl.when(here & (p % 2 == 0) & (p + 2 < tp))
        def _():
            act(gat_copy(source, c, way, 1))

        @pl.when(here & (((p % 2 == 0) | (source == z)) & (p + 1 < tp)))
        def _():
            act(gat_copy(source, c, way, 0))

    def gat_own(c, act=lambda copy: copy.start()):
        for way in range(2):
            gat_pass(z, c, way, z >= 0, act)

    def gat_more(c, j, act=lambda copy: copy.start()):
        source = near(j)
        gat_pass(source, c, 0, source < z, act)
        gat_pass(source, c, 1, source > z, act)

    def gat_step(c, j):
        gat_copy(near(j), c, 0, 0).wait_recv()
        gat_more(c, j)

    def project(source, h, start):
        term = jnp.dot(
            gat[source, h], wfull[source].reshape(chans, wide), preferred_element_type=f32
        )
        if start:
            hacc[...] = term
        else:
            hacc[...] += term

    def all_terms(h):
        hyena = hacc[...].astype(jnp.bfloat16)
        hyena_ref[h * half : (h + 1) * half, :] = hyena
        for d in range(tp):
            own_terms[h, d] = jnp.dot(
                hyena_ref[h * half : (h + 1) * half, :], vv[d], preferred_element_type=f32
            )

    def sum_rows(c):
        tall = half // SUM_CUTS
        return pl.ds(c % SUM_CUTS * tall, tall)

    def sum_copy(d, c, way, hop):
        h, at = c // SUM_CUTS, sum_rows(c)
        return remote(
            snd.at[h, d, at, :],
            boxes.at[way, hop - 1, h, d, at, :],
            sum_send.at[c, d],
            sum_recv.at[c, way, hop - 1, d],
            {"tp": jnp.clip(z + hop * (1 - 2 * way), 0, tp - 1)},
        )

    def sum_add(d, c, way, hop):
        h, at = c // SUM_CUTS, sum_rows(c)

        @pl.when(place_of(way) >= hop)
        def _():
            sum_copy(d, c, way, hop).wait_recv()
            own_terms[h, d, at, :] += boxes[way, hop - 1, h, d, at, :].astype(f32)

    def sum_hop(k, way):
        return jnp.where(place_of(way) % 2 == 1, min(k, 2), 1)

    def sum_step(c, k, odd):
        h, at = c // SUM_CUTS, sum_rows(c)
        for way in range(2):
            d = z + k * (1 - 2 * way)
            p = place_of(way)

            @pl.when((p + k < tp) & (p % 2 == odd))
            def _():
                if odd:
                    sum_add(d, c, way, 1)
                    if tp > 4:
                        sum_add(d, c, way, 2)
                snd[h, d, at, :] = own_terms[h, d, at, :].astype(jnp.bfloat16)
                sum_copy(d, c, way, sum_hop(k, way)).start()

    def sum_last(h):
        for c in range(h * SUM_CUTS, (h + 1) * SUM_CUTS):
            for way in range(2):
                sum_add(z, c, way, 1)

                @pl.when(place_of(way) % 2 == 1)
                def _():
                    sum_add(z, c, way, 2)

        vals[me, h] = own_terms[h, z].astype(jnp.bfloat16)
        val_parts[h].own()

    scale = math.log2(math.e) / math.sqrt(HD)

    def weigh(head):
        here = slice(head * HD, (head + 1) * HD)

        def score(b):
            return (
                lax.dot_general(
                    q_ref[:, here], keys[b, :, here], (((1,), (1,)), ((), ())), preferred_element_type=f32
                )
                * scale
            )

        def fold(value, act):
            part = value[:, :HD]
            for at in range(HD, rows, HD):
                part = act(part, value[:, at : at + HD])
            return part

        query = lax.broadcasted_iota(jnp.int32, (rows, rows), 0)
        key = lax.broadcasted_iota(jnp.int32, (rows, rows), 1)
        mine = jnp.where(key <= query, score(me), -1e30)
        scores[me] = mine
        tops[...] = fold(mine, jnp.maximum)

        def earlier(b):
            value = score(b)
            scores[b] = value
            tops[...] = jnp.maximum(tops[...], fold(value, jnp.maximum))

        each(me, earlier)
        top = jnp.max(tops[...], axis=1, keepdims=True)
        tops[...] = jnp.broadcast_to(top, tops.shape)
        totals[head] = jnp.zeros_like(tops)

        def weight(b):
            value = jnp.exp2(scores[b] - tops[:, 0:1])
            totals[head] += fold(value, jnp.add)
            probs[head, b] = value.astype(jnp.bfloat16)

        each(me + 1, weight)
        totals[head] = jnp.broadcast_to(jnp.sum(totals[head], axis=1, keepdims=True), tops.shape)

    def blend():
        def step(b, sums):
            return tuple(
                sums[head]
                + jnp.dot(
                    probs[head, b],
                    vals[b, :, :, head * HD : (head + 1) * HD].reshape(rows, HD),
                    preferred_element_type=f32,
                )
                for head in range(heads)
            )

        sums = lax.fori_loop(0, me + 1, step, (jnp.zeros((rows, HD), f32),) * heads)
        for head in range(heads):
            out_ref[:, head * HD : (head + 1) * HD] = (sums[head] / totals[head]).astype(jnp.bfloat16)

    gat_own(0)
    key_part.relay_first()
    w_own(1, True)
    w_each(0, Gather.relay_first)
    key_part.relay_second()
    key_part.take()
    loads[6].wait()
    weigh(0)
    w_each(0, Gather.relay_second)
    w_each(1, Gather.relay_first)
    for load in loads[7:]:
        load.wait()
    project(z, 0, True)
    for j in others[2:]:
        w_own(j, False)
    gat_step(0, 0)
    gat_own(1)
    weigh(1)
    w_each(1, Gather.relay_second)
    w_each(0, Gather.take)
    project(near(0), 0, False)
    gat_step(0, 1)
    w_each(1, Gather.take)
    project(near(1), 0, False)
    for j in others[2:]:
        w_each(j, Gather.relay)
        gat_step(0, j)
        w_each(j, Gather.take)
        project(near(j), 0, False)
    all_terms(0)
    for k in reversed(hops):
        sum_step(0, k, 0)
    gat_step(1, 0)
    gat_step(1, 1)
    weigh(2) if heads > 2 else None
    for k in reversed(hops):
        sum_step(0, k, 1)
    for j in others[2:]:
        gat_step(1, j)
    project(z, 1, True)
    for j in others:
        project(near(j), 1, False)
    all_terms(1)
    for k in reversed(hops):
        sum_step(1, k, 0)
    sum_last(0)
    for head in range(3, heads):
        weigh(head)
    for k in reversed(hops):
        sum_step(1, k, 1)
    val_parts[0].relay()
    sum_last(1)
    val_parts[0].take()
    val_parts[1].relay()
    val_parts[1].take()
    blend()

    @pl.when(me < ctx - 1)
    def _():
        halo.wait_send()

    each(ctx - 1 - me, lambda i: end_copy(i + 1).wait_send())
    for j in others:
        for r in range(w_cuts):
            w_copy(j, r).wait_send()
        w_each(j, Gather.finish)
    key_part.finish()
    for h in range(HALVES):
        val_parts[h].finish()
    for c in range(HALVES * GAT_CUTS):
        gat_own(c, lambda copy: copy.wait_send())
        for j in others:
            gat_more(c, j, lambda copy: copy.wait_send())
    for c in range(HALVES * SUM_CUTS):
        for k in hops:
            for way in range(2):

                @pl.when(place_of(way) + k < tp)
                def _():
                    sum_copy(z + k * (1 - 2 * way), c, way, 1).wait_send()


def shards(streams, short_filter, decay_rates, residues, skip_gain, hyena_weight, value_weight, queries, key_vectors):
    ctx, tp = lax.axis_size("ctx"), lax.axis_size("tp")
    rows, chans = streams.shape[1:]
    width = queries.shape[1]
    wide = hyena_weight.shape[1] // tp
    deep = value_weight.shape[0]
    part = chans // ctx
    modes = decay_rates.shape[1]
    taps = short_filter.shape[1]
    blocks = chans // LANES
    heads = width // HD
    half = rows // HALVES
    f32, bf16 = jnp.float32, jnp.bfloat16
    dma = pltpu.SemaphoreType.DMA
    vmem = pltpu.VMEM
    return pl.pallas_call(
        functools.partial(body, ctx, tp),
        in_specs=[pl.BlockSpec(memory_space=pltpu.HBM)] * 9,
        out_specs=[pl.BlockSpec(memory_space=pltpu.VMEM)] * 2,
        out_shape=[
            jax.ShapeDtypeStruct((rows, wide), bf16),
            jax.ShapeDtypeStruct((rows, width), bf16),
        ],
        scratch_shapes=[
            vmem((3, rows, chans), bf16),
            vmem((3, HALO, chans), bf16),
            vmem((3, taps, chans), f32),
            vmem((modes, chans), f32),
            vmem((modes, chans), f32),
            vmem((1, chans), f32),
            vmem((3, rows + HALO, LANES), f32),
            vmem((blocks, rows, LANES), f32),
            vmem((blocks, rows, LANES), f32),
            vmem((blocks, modes * SEGS, LANES), f32),
            vmem((modes * SEGS, LANES), f32),
            vmem((ctx, blocks, modes, LANES), f32),
            vmem((tp, HALVES, half, chans), bf16),
            vmem((tp, part, wide), bf16),
            vmem((tp, ctx, part, wide), bf16),
            vmem((tp, deep, width), bf16),
            vmem((rows, width), bf16),
            vmem((ctx, rows, width), bf16),
            vmem((ctx, HALVES, half, width), bf16),
            vmem((half, wide), f32),
            vmem((HALVES, tp, half, width), f32),
            vmem((HALVES, tp, half, width), bf16),
            vmem((2, 2, HALVES, tp, half, width), bf16),
            vmem((ctx, rows, rows), f32),
            vmem((heads, ctx, rows, rows), bf16),
            vmem((rows, HD), f32),
            vmem((heads, rows, HD), f32),
            dma((8 + 2 * tp,)),
            dma((2,)),
            dma((2, ctx)),
            dma((2, W_CUTS, tp)),
            dma((W_CUTS, tp, ctx)),
            dma((W_CUTS, tp, ctx)),
            dma((ctx,)),
            dma((ctx,)),
            dma((HALVES, ctx)),
            dma((HALVES, ctx)),
            dma((HALVES * GAT_CUTS, 2, 2, tp)),
            dma((HALVES * GAT_CUTS, tp)),
            dma((HALVES * SUM_CUTS, tp)),
            dma((HALVES * SUM_CUTS, 2, 2, tp)),
        ],
        cost_estimate=pl.CostEstimate(
            flops=4 * rows * ctx * rows * width,
            bytes_accessed=4 * ctx * rows * width,
            transcendentals=0,
        ),
        compiler_params=pltpu.CompilerParams(
            vmem_limit_bytes=56 * 1024 * 1024, collective_id=0, has_side_effects=True
        ),
        name="hyena_attention",
    )(
        streams,
        short_filter,
        decay_rates.T,
        residues.T,
        skip_gain[None],
        hyena_weight.reshape(ctx, part, tp * wide),
        value_weight,
        queries,
        key_vectors,
    )


def solution(mesh):
    return jax.shard_map(
        shards,
        mesh=mesh,
        in_specs=(
            P(None, "ctx", "tp"),
            P(None, None, "tp"),
            P("tp", None),
            P("tp", None),
            P("tp"),
            P("tp", None),
            P("tp", None),
            P("ctx", "tp"),
            P("ctx", "tp"),
        ),
        out_specs=(P("ctx", "tp"), P("ctx", "tp")),
        check_vma=False,
    )
```
